128 devices in a mesh: row: 8 (over y, core), col: 16 (over z, x).
Axes of the slice: x: 4, y: 4, z: 4, core: 2. Of those that a mesh axis runs over, the one named last changes fastest.
Arguments:
- right_side: float32 [2, 8, 512, 4096], P(None, 'row', None, 'col'), may hold values from -6 to 6
- factor_store: bfloat16 [2, 8, 512, 16, 1, 512], P(None, 'row', None, 'col'), may hold values from -0.125 to 0.125
- col_owner: int32 [16], replicated, may hold values from 0 to 15, each once
- window_start: int32 [1], replicated, may hold values from 0 to 8
- stress_kernel: bfloat16 [8, 512, 768], replicated, may hold values from -0.09375 to 0.09375
Outputs:
- solution: float32 [2, 8, 512, 4096], P(None, 'row', None, 'col')
- stress: float32 [4096, 768], P(('col', 'row'))
The draws below stay inside these ranges and needn't reach their ends.
Inputs may be any that keep to these rules, and one draw needn't show every extreme that they name: col_owner is a permutation of 0 .. 15.
All inputs are finite; a program needn't handle non-finite values.
Results may differ from the reference program's by a relative error of at most 0.013.
Values may be sent and summed in bfloat16 or wider, within the bound.
No kernel may reach another device: no remote copies, remote signals or barrier semaphores. Data moves between devices by JAX's collectives and lax.ppermute only.
A program may use at most 128 MiB of HBM per device.

```python
import jax
import jax.numpy as jnp
from jax import lax

NB = 512
STEPS = 8
ROWP_DEV = 2
COLP_DEV = 1
CASES = 4096
STRESS_COLS = 768
N_ROW = 8
N_COL = 16


def shard_levels(stream_key, shape, pieces, least, largest):
    level, own = 1.0, jax.random.fold_in(stream_key, 6)
    for axis_at, shards_of in pieces:
        draws = jnp.exp(jax.random.uniform(jax.random.fold_in(own, axis_at), (shards_of,), jnp.float32, least / len(pieces), largest / len(pieces)))
        level = level * jnp.repeat(draws, shape[axis_at] // shards_of).reshape([-1 if axis == axis_at else 1 for axis in range(len(shape))])
    return level


def normal_values(stream_key, extent, deviation, reach, split=(), held_as=jnp.bfloat16):
    array = deviation * jax.random.normal(stream_key, extent, jnp.float32)
    if split:
        array = array * shard_levels(stream_key, extent, split, -0.22, 0.18)
    return jnp.clip(array, -reach, reach).astype(held_as)


def setup_inputs(seed: int = 0) -> dict:
    splits = jax.random.split(jax.random.key(seed), 6)
    return {
        "right_side": normal_values(splits[0], (ROWP_DEV, N_ROW, NB, CASES), 1.0, 6.0, ((1, 8), (3, 16)), jnp.float32),
        "factor_store": normal_values(splits[1], (ROWP_DEV, N_ROW, NB, N_COL, COLP_DEV, NB), (4 * NB) ** -0.5, 0.125, ((1, 8), (3, 16))),
        "col_owner": jax.random.permutation(splits[2], N_COL).astype(jnp.int32),
        "window_start": jax.random.randint(splits[3], (1,), 0, N_ROW * ROWP_DEV - STEPS + 1).astype(jnp.int32),
        "stress_kernel": normal_values(splits[4], (STEPS, NB, STRESS_COLS), (STEPS * NB) ** -0.5, 0.09375),
    }


def column_panel(store, col_owner, block_col, panels):
    owner_index = col_owner[block_col % N_COL]
    part_cols = lax.dynamic_index_in_dim(store, owner_index, 3, keepdims=False)
    part_cols = lax.dynamic_index_in_dim(part_cols, block_col // N_COL, 3, keepdims=False)
    return part_cols.reshape(panels, NB, NB)


def one_step(system_state, store, col_owner, block_col, numbers, panels, later):
    panel_rows = column_panel(store, col_owner, block_col, panels)
    rows_now = lax.dynamic_index_in_dim(system_state, block_col, 0, keepdims=False)
    if later:
        solved = rows_now.astype(jnp.bfloat16)
    else:
        diagonal = lax.dynamic_index_in_dim(panel_rows, block_col, 0, keepdims=False)
        solved = jnp.dot(diagonal, rows_now.astype(jnp.bfloat16), preferred_element_type=jnp.float32).astype(jnp.bfloat16)
    solved = lax.optimization_barrier(solved)
    change = jnp.einsum("gts,sc->gtc", panel_rows.astype(jnp.float32), solved.astype(jnp.float32), precision=lax.Precision.HIGHEST)
    if later:
        selected = numbers > block_col
    else:
        selected = numbers < block_col
    system_state = jnp.where(selected[:, None, None], system_state - change, system_state)
    return lax.dynamic_update_index_in_dim(system_state, solved.astype(jnp.float32)[None], block_col, 0)


def reference(right_side, factor_store, col_owner, window_start, stress_kernel):
    panels = ROWP_DEV * N_ROW
    system_state = right_side.reshape(panels, NB, CASES)
    first_panel = window_start[0]
    numbers = jnp.arange(panels, dtype=jnp.int32)
    for section in range(STEPS):
        system_state = one_step(system_state, factor_store, col_owner, first_panel + section, numbers, panels, True)
    for section in range(STEPS):
        system_state = one_step(system_state, factor_store, col_owner, first_panel + STEPS - 1 - section, numbers, panels, False)
    window = lax.dynamic_slice_in_dim(system_state, first_panel, STEPS, 0).reshape(STEPS * NB, CASES).astype(jnp.bfloat16)
    stress = jnp.dot(window.T, stress_kernel.reshape(STEPS * NB, STRESS_COLS), preferred_element_type=jnp.float32)
    return system_state.reshape(ROWP_DEV, N_ROW, NB, CASES), stress
```

```python
import jax
import jax.numpy as jnp
from jax import lax
from jax.experimental import pallas as pl
from jax.experimental.pallas import tpu as pltpu
from jax.sharding import PartitionSpec as P

STEPS = 8
BF16 = jnp.bfloat16
F32 = jnp.float32


def nt_dot(a, b):
    return lax.dot_general(a, b, (((1,), (1,)), ((), ())), preferred_element_type=F32)


def window_solve_kernel(start_ref, load_ref, factor_ref, forward_ref, back_ref, blocks, state, sems):
    first = start_ref[0]
    panels = [(p, k) for k in range(STEPS) for p in range(k + 1, STEPS)]
    panels += [(p, k) for k in range(STEPS - 1, -1, -1) for p in range(k, -1, -1)]
    copies = {}
    for p, k in panels:
        source = factor_ref.at[lax.rem(first + p, STEPS), :, k]
        copies[p, k] = pltpu.make_async_copy(source, blocks.at[p, k], sems.at[p, k])
        copies[p, k].start()
    for p in range(STEPS):
        state[p] = load_ref[lax.rem(first + p, STEPS)]

    def block(p, k):
        copies[p, k].wait()
        value = blocks[p, k]
        return value.reshape(value.shape[0] * value.shape[1], value.shape[2])

    for k in range(STEPS):
        solved = state[k].astype(BF16)
        state[k] = solved.astype(F32)
        forward_ref[k] = solved
        for p in range(k + 1, STEPS):
            state[p] = state[p] - nt_dot(solved, block(p, k))
    for k in range(STEPS - 1, -1, -1):
        solved = nt_dot(state[k].astype(BF16), block(k, k)).astype(BF16)
        back_ref[k] = solved
        for p in range(k - 1, -1, -1):
            state[p] = state[p] - nt_dot(solved, block(p, k))


def window_solve(window_start, load, factor):
    rows_n, cases, width = load.shape
    out = jax.ShapeDtypeStruct((STEPS, cases, width), BF16)
    whole = pl.BlockSpec(memory_space=pltpu.VMEM)
    return pl.pallas_call(
        window_solve_kernel,
        out_shape=(out, out),
        in_specs=[pl.BlockSpec(memory_space=pltpu.SMEM), whole, pl.BlockSpec(memory_space=pl.ANY)],
        out_specs=(whole, whole),
        scratch_shapes=[
            pltpu.VMEM((STEPS, STEPS) + factor.shape[1:2] + factor.shape[3:], BF16),
            pltpu.VMEM((STEPS, cases, width), F32),
            pltpu.SemaphoreType.DMA((STEPS, STEPS)),
        ],
        compiler_params=pltpu.CompilerParams(vmem_limit_bytes=56 * 2**20),
        cost_estimate=pl.CostEstimate(
            flops=2 * 64 * width * width * cases, bytes_accessed=64 * width * width * 2, transcendentals=0
        ),
        name="window_solve",
    )(window_start, load, factor)


def shards(right_side, factor_store, col_owner, window_start, stress_kernel):
    rows_n = lax.axis_size("row")
    cols_n = lax.axis_size("col")
    row_id = lax.axis_index("row")
    first = window_start[0]
    panels_dev, _, width, cases = right_side.shape
    own_cases = cases // rows_n
    slice_rows = width // cols_n
    rank = (row_id - first) % rows_n
    inside = (first + rank) // rows_n
    state = right_side.reshape(panels_dev, width, cases)
    factor = factor_store.reshape(panels_dev, width, width)

    ranks = jnp.arange(STEPS, dtype=jnp.int32)
    owners = jnp.take(col_owner, (first + ranks) % cols_n)

    def spread(panel):
        parts = panel.reshape(cols_n, slice_rows, width)
        parts = lax.all_to_all(parts, "col", 0, 0)
        return jnp.stack(
            [lax.dynamic_index_in_dim(parts, owners[k], 0, keepdims=False) for k in range(STEPS)]
        )

    window_factor = lax.dynamic_index_in_dim(factor, inside, 0, keepdims=False)
    outer_factor = lax.dynamic_index_in_dim(factor, 1 - inside, 0, keepdims=False)
    gathered = lax.all_gather(spread(window_factor), ("row", "col"))
    gathered = gathered.reshape(rows_n, cols_n, STEPS, slice_rows, width)
    outer_gathered = lax.all_gather(spread(outer_factor), "col")

    window_load = lax.dynamic_index_in_dim(state, inside, 0, keepdims=False)
    outer_load = lax.dynamic_index_in_dim(state, 1 - inside, 0, keepdims=False)
    load = window_load.T.reshape(rows_n, own_cases, width)
    load = lax.all_to_all(load, "row", 0, 0)

    forward, back = window_solve(window_start, load, gathered)

    stress = jnp.einsum("kcu,kus->cs", back, stress_kernel, preferred_element_type=F32)

    target_rank = (jnp.arange(rows_n, dtype=jnp.int32) - first) % rows_n
    target_upper = (first + target_rank) // rows_n == 1
    outgoing = []
    for target in range(rows_n):
        used = jnp.where(target_upper[target], back, forward)
        own = lax.dynamic_index_in_dim(back, target_rank[target], 0, keepdims=True)
        outgoing.append(jnp.concatenate([used, own]))
    arrived = lax.all_to_all(jnp.stack(outgoing), "row", 0, 0)
    used = arrived[:, :STEPS]
    window_out = arrived[:, STEPS].reshape(cases, width).T.astype(F32)
    change = jnp.einsum("jktu,nkcu->jtnc", outer_gathered, used, preferred_element_type=F32)
    outer_out = outer_load - change.reshape(width, cases)
    low = inside == 0
    result = jnp.stack([jnp.where(low, window_out, outer_out), jnp.where(low, outer_out, window_out)])
    return result.reshape(right_side.shape), stress


def solution(mesh):
    in_specs = (P(None, "row", None, "col"), P(None, "row", None, "col", None, None), P(), P(), P())
    out_specs = (P(None, "row", None, "col"), P(("col", "row"), None))
    return jax.shard_map(shards, mesh=mesh, in_specs=in_specs, out_specs=out_specs, check_vma=False)
```

```python
import jax
import jax.numpy as jnp
from jax import lax
from jax.experimental import pallas as pl
from jax.experimental.pallas import tpu as pltpu
from jax.sharding import PartitionSpec as P

STEPS = 8
HALF = STEPS // 2
CHIPS_Y = 4
CORES = 2
BF16 = jnp.bfloat16
F32 = jnp.float32


def dot_nn(a, b):
    return lax.dot_general(a, b, (((1,), (0,)), ((), ())), preferred_element_type=F32)


def dot_nt(a, b):
    return lax.dot_general(a, b, (((1,), (1,)), ((), ())), preferred_element_type=F32)


def start_blocks(first, factor_ref, blocks, sems, panels):
    copies = {}
    for p, k in panels:
        source = factor_ref.at[lax.rem(first + p, STEPS), :, k]
        copies[p, k] = pltpu.make_async_copy(source, blocks.at[p, k], sems.at[p, k])
        copies[p, k].start()

    def block(p, k):
        copies[p, k].wait()
        value = blocks[p, k]
        return value.reshape(value.shape[0] * value.shape[1], value.shape[2])

    return block


def forward_kernel(start_ref, load_ref, factor_ref, solved_ref, blocks, state, sems):
    first = start_ref[0]
    panels = [(p, k) for k in range(STEPS) for p in range(k + 1, STEPS)]
    block = start_blocks(first, factor_ref, blocks, sems, panels)
    for p in range(STEPS):
        state[p] = load_ref[lax.rem(first + p, STEPS)]
    for k in range(STEPS):
        solved = state[k].astype(BF16)
        solved_ref[k] = solved
        for p in range(k + 1, STEPS):
            state[p] = state[p] - dot_nn(solved, block(p, k))


def backward_kernel(start_ref, forward_ref, factor_ref, solved_ref, blocks, state, sems):
    first = start_ref[0]
    panels = [(p, k) for k in range(STEPS - 1, -1, -1) for p in range(k, -1, -1)]
    block = start_blocks(first, factor_ref, blocks, sems, panels)
    for p in range(STEPS):
        state[p] = forward_ref[p].astype(F32)
    for k in range(STEPS - 1, -1, -1):
        solved = dot_nn(state[k].astype(BF16), block(k, k)).astype(BF16)
        solved_ref[k] = solved
        for p in range(k - 1, -1, -1):
            state[p] = state[p] - dot_nn(solved, block(p, k))


def substitution(kernel, name, blocks_n, window_start, rows, factor):
    _, cases, width = rows.shape
    whole = pl.BlockSpec(memory_space=pltpu.VMEM)
    return pl.pallas_call(
        kernel,
        out_shape=jax.ShapeDtypeStruct((STEPS, cases, width), BF16),
        in_specs=[pl.BlockSpec(memory_space=pltpu.SMEM), whole, pl.BlockSpec(memory_space=pl.ANY)],
        out_specs=whole,
        scratch_shapes=[
            pltpu.VMEM((STEPS, STEPS) + factor.shape[1:2] + factor.shape[3:], BF16),
            pltpu.VMEM((STEPS, cases, width), F32),
            pltpu.SemaphoreType.DMA((STEPS, STEPS)),
        ],
        compiler_params=pltpu.CompilerParams(vmem_limit_bytes=48 * 2**20),
        cost_estimate=pl.CostEstimate(
            flops=2 * blocks_n * width * width * cases,
            bytes_accessed=blocks_n * width * width * 2,
            transcendentals=0,
        ),
        name=name,
    )(window_start, rows, factor)


def origin_xor(bits, core):
    mask = 0
    if bits & 1:
        mask = jnp.where(core == 0, 1, 3)
    if bits & 2:
        mask = mask ^ jnp.where(core == 0, 3, 1)
    return mask


def outer_kernel(place_ref, *refs):
    forward_pieces = refs[0:CHIPS_Y]
    back_pieces = refs[CHIPS_Y : 2 * CHIPS_Y]
    factor_slots = (refs[2 * CHIPS_Y : 2 * CHIPS_Y + 2], refs[2 * CHIPS_Y + 2 : 2 * CHIPS_Y + 4])
    keep_ref, send_ref, factor, used, solved, factor_sem, used_sem, solved_sem = refs[2 * CHIPS_Y + 4 :]
    first, y, core, z, x = (place_ref[i] for i in range(5))
    rows_n = CHIPS_Y * CORES
    factor_copies = ([], [])
    for rb in range(CORES):
        for half in range(2):
            for low in range(8):
                slot = half * 8 + low
                near, far = origin_xor(slot & 3, core), origin_xor(slot >> 2, core)
                if rb == 0:
                    place = (z ^ far) * 4 + (x ^ near)
                else:
                    place = (z ^ near) * 4 + (x ^ far)
                copy = pltpu.make_async_copy(
                    factor_slots[rb][half].at[low], factor.at[rb, :, place], factor_sem.at[rb, slot]
                )
                copy.start()
                factor_copies[rb].append(copy)
    used_copies = ([], [])
    for rb in range(CORES):
        upper = CORES * y + rb < first
        for shift in range(CHIPS_Y):
            chip = lax.rem(y - shift + CHIPS_Y, CHIPS_Y)
            for side in range(CORES):
                place = chip * CORES + (side ^ core)
                target = used.at[rb, :, place]
                sem = used_sem.at[rb, shift, side]
                back = pltpu.make_async_copy(back_pieces[shift].at[side], target, sem)
                fore = pltpu.make_async_copy(forward_pieces[shift].at[side], target, sem)

                @pl.when(upper)
                def _(back=back):
                    back.start()

                @pl.when(jnp.logical_not(upper))
                def _(fore=fore):
                    fore.start()

                used_copies[rb].append(back)
    solved_copies = []
    for which in range(CORES):
        row = CORES * y + (core ^ which)
        rank = lax.rem(row - first + rows_n, rows_n)
        column = lax.rem(rank, HALF)
        for shift in range(CHIPS_Y):
            chip = lax.rem(y - shift + CHIPS_Y, CHIPS_Y)
            for side in range(CORES):
                place = chip * CORES + (side ^ core)
                copy = pltpu.make_async_copy(
                    back_pieces[shift].at[side, column], solved.at[which, place], solved_sem.at[which, shift, side]
                )
                copy.start()
                solved_copies.append(copy)
    for copies in factor_copies + used_copies:
        for copy in copies:
            copy.wait()
    for which, target in ((1, send_ref), (0, keep_ref)):
        rb = core ^ which
        total = None
        for k in range(HALF):
            left = factor[rb, k]
            right = used[rb, k]
            left = left.reshape(left.shape[0] * left.shape[1], left.shape[2])
            right = right.reshape(right.shape[0] * right.shape[1], right.shape[2])
            term = dot_nt(left, right)
            total = term if total is None else total + term
        target[0] = total
    for copy in solved_copies:
        copy.wait()
    for which, target in ((1, send_ref), (0, keep_ref)):
        panel = solved[which]
        panel = panel.reshape(panel.shape[0] * panel.shape[1], panel.shape[2])
        target[1] = jnp.transpose(panel.astype(F32))


def outer_product(place, forward_pieces, back_pieces, factor_slots):
    _, _, cases, width = forward_pieces[0].shape
    slices, slice_rows = 16, factor_slots[0].shape[2]
    all_cases = CHIPS_Y * CORES * cases
    out = jax.ShapeDtypeStruct((2, width, all_cases), F32)
    whole = pl.BlockSpec(memory_space=pltpu.VMEM)
    remote = pl.BlockSpec(memory_space=pl.ANY)
    return pl.pallas_call(
        outer_kernel,
        out_shape=(out, out),
        in_specs=[pl.BlockSpec(memory_space=pltpu.SMEM)] + [remote] * (2 * CHIPS_Y + 4),
        out_specs=(whole, whole),
        scratch_shapes=[
            pltpu.VMEM((CORES, HALF, slices, slice_rows, width), BF16),
            pltpu.VMEM((CORES, HALF, CHIPS_Y * CORES, cases, width), BF16),
            pltpu.VMEM((CORES, CHIPS_Y * CORES, cases, width), BF16),
            pltpu.SemaphoreType.DMA((CORES, slices)),
            pltpu.SemaphoreType.DMA((CORES, CHIPS_Y, CORES)),
            pltpu.SemaphoreType.DMA((CORES, CHIPS_Y, CORES)),
        ],
        compiler_params=pltpu.CompilerParams(vmem_limit_bytes=32 * 2**20),
        cost_estimate=pl.CostEstimate(
            flops=2 * CORES * HALF * width * width * all_cases,
            bytes_accessed=CORES * HALF * width * (width + all_cases) * 2,
            transcendentals=0,
        ),
        name="outer_product",
    )(place, *forward_pieces, *back_pieces, *factor_slots)


def device_pairs(move):
    pairs = []
    for y in range(4):
        for core in range(2):
            for z in range(4):
                for x in range(4):
                    to_y, to_core, to_z, to_x = move(y, core, z, x)
                    pairs.append(((y * 2 + core) * 16 + z * 4 + x, (to_y * 2 + to_core) * 16 + to_z * 4 + to_x))
    return pairs


def double(value, axis, step):
    masks = (1, 3) if step == 0 else (3, 1)

    def move(y, core, z, x):
        if axis == "x":
            return y, core, z, x ^ masks[core]
        return y, core, z ^ masks[core], x

    return lax.ppermute(value, ("row", "col"), device_pairs(move))


def swap_cores(value):
    return lax.ppermute(value, "row", [(r, r ^ 1) for r in range(CHIPS_Y * CORES)])


def round_y(value):
    rows = [(y, core) for y in range(CHIPS_Y) for core in range(CORES)]
    pieces = [value]
    for shift in range(1, CHIPS_Y):
        pairs = [(y * CORES + core, (y + shift) % CHIPS_Y * CORES + core) for y, core in rows]
        pieces.append(lax.ppermute(value, "row", pairs))
    return pieces


def own_half(value, core):
    kept = lax.dynamic_slice_in_dim(value, core * HALF, HALF, 0)
    sent = lax.dynamic_slice_in_dim(value, (1 - core) * HALF, HALF, 0)
    return jnp.stack([kept, swap_cores(sent)])


def gather_outer(slices, core):
    both = own_half(slices, core)
    first_row = jnp.where(core == 0, both[0], both[1])[None]
    second_row = jnp.where(core == 0, both[1], both[0])[None]
    parts = [first_row, second_row]
    orders = (("x", "x", "z", "z"), ("z", "z", "x", "x"))
    for step in range(4):
        got = [double(part, orders[i][step], step % 2) for i, part in enumerate(parts)]
        if step == 3:
            return [parts[0], got[0], parts[1], got[1]]
        parts = [jnp.concatenate([part, new]) for part, new in zip(parts, got)]


def shards(right_side, factor_store, col_owner, window_start, stress_kernel):
    rows_n = lax.axis_size("row")
    cols_n = lax.axis_size("col")
    row_id = lax.axis_index("row")
    col_id = lax.axis_index("col")
    core = row_id % CORES
    first = window_start[0]
    panels_dev, _, width, cases = right_side.shape
    own_cases = cases // rows_n
    slice_rows = width // cols_n
    rank = (row_id - first) % rows_n
    inside = (first + rank) // rows_n
    state = right_side.reshape(panels_dev, width, cases)
    factor = factor_store.reshape(panels_dev, width, width)

    ranks = jnp.arange(STEPS, dtype=jnp.int32)
    owners = jnp.take(col_owner, (first + ranks) % cols_n)

    def spread(panel):
        parts = panel.reshape(cols_n, slice_rows, width)
        parts = lax.all_to_all(parts, "col", 0, 0)
        return jnp.stack(
            [lax.dynamic_index_in_dim(parts, owners[k], 0, keepdims=False) for k in range(STEPS)]
        )

    window_factor = lax.dynamic_index_in_dim(factor, inside, 0, keepdims=False)
    outer_factor = lax.dynamic_index_in_dim(factor, 1 - inside, 0, keepdims=False)
    gathered = lax.all_gather(spread(window_factor.T), ("row", "col"))
    gathered = gathered.reshape(rows_n, cols_n, STEPS, slice_rows, width)

    window_load = lax.dynamic_index_in_dim(state, inside, 0, keepdims=False)
    outer_load = lax.dynamic_index_in_dim(state, 1 - inside, 0, keepdims=False)
    load = window_load.T.reshape(rows_n, own_cases, width)
    load = lax.all_to_all(load, "row", 0, 0)
    factor_slots = gather_outer(spread(outer_factor), core)

    forward = substitution(forward_kernel, "forward", 28, window_start, load, gathered)
    forward_pieces = round_y(own_half(forward, core))
    back = substitution(backward_kernel, "backward", 36, window_start, forward, gathered)
    back_pieces = round_y(own_half(back, core))

    stress = jnp.einsum("kcu,kus->cs", back, stress_kernel, preferred_element_type=F32)

    place = jnp.stack([first, row_id // CORES, core, col_id // 4, col_id % 4]).astype(jnp.int32)
    kept, sent = outer_product(place, forward_pieces, back_pieces, factor_slots)
    got = swap_cores(sent)
    outer_out = outer_load - kept[0] - got[0]
    window_out = jnp.where(rank // HALF == core, kept[1], got[1])
    low = inside == 0
    result = jnp.stack([jnp.where(low, window_out, outer_out), jnp.where(low, outer_out, window_out)])
    return result.reshape(right_side.shape), stress


def solution(mesh):
    in_specs = (P(None, "row", None, "col"), P(None, "row", None, "col", None, None), P(), P(), P())
    out_specs = (P(None, "row", None, "col"), P(("col", "row"), None))
    return jax.shard_map(shards, mesh=mesh, in_specs=in_specs, out_specs=out_specs, check_vma=False)
```

```python
import jax
import jax.numpy as jnp
from jax import lax
from jax.experimental import pallas as pl
from jax.experimental.pallas import tpu as pltpu
from jax.sharding import PartitionSpec as P

STEPS = 8
HALF = STEPS // 2
CHIPS_Y = 4
CORES = 2
BF16 = jnp.bfloat16
F32 = jnp.float32


def dot_nn(a, b):
    return lax.dot_general(a, b, (((1,), (0,)), ((), ())), preferred_element_type=F32)


def dot_nt(a, b):
    return lax.dot_general(a, b, (((1,), (1,)), ((), ())), preferred_element_type=F32)


def start_blocks(first, factor_ref, blocks, sems, panels):
    slots = {panel: slot for slot, panel in enumerate(panels)}
    copies = {}
    for p, k in panels:
        slot = slots[p, k]
        source = factor_ref.at[lax.rem(first + p, STEPS), :, k]
        copies[p, k] = pltpu.make_async_copy(source, blocks.at[slot], sems.at[slot])
        copies[p, k].start()

    def block(p, k):
        copies[p, k].wait()
        value = blocks[slots[p, k]]
        return value.reshape(value.shape[0] * value.shape[1], value.shape[2])

    return block


def forward_kernel(place_ref, load_ref, factor_ref, solved_ref, halves_ref, blocks, state, sems):
    first, core = place_ref[0], place_ref[2]
    panels = [(p, k) for k in range(STEPS) for p in range(k + 1, STEPS)]
    block = start_blocks(first, factor_ref, blocks, sems, panels)
    for p in range(STEPS):
        state[p] = load_ref[lax.rem(first + p, STEPS)]
    for k in range(STEPS):
        solved = state[k].astype(BF16)
        solved_ref[k] = solved
        halves_ref[(k // HALF) ^ core, k % HALF] = solved
        for p in range(k + 1, STEPS):
            state[p] = state[p] - dot_nn(solved, block(p, k))


def backward_kernel(place_ref, forward_ref, factor_ref, solved_ref, halves_ref, blocks, state, sems):
    first, core = place_ref[0], place_ref[2]
    panels = [(p, k) for k in range(STEPS - 1, -1, -1) for p in range(k, -1, -1)]
    block = start_blocks(first, factor_ref, blocks, sems, panels)
    for p in range(STEPS):
        state[p] = forward_ref[p].astype(F32)
    for k in range(STEPS - 1, -1, -1):
        solved = dot_nn(state[k].astype(BF16), block(k, k)).astype(BF16)
        solved_ref[k] = solved
        halves_ref[(k // HALF) ^ core, k % HALF] = solved
        for p in range(k - 1, -1, -1):
            state[p] = state[p] - dot_nn(solved, block(p, k))


def substitution(kernel, name, blocks_n, cost, place, rows, factor):
    _, cases, width = rows.shape
    whole = pl.BlockSpec(memory_space=pltpu.VMEM)
    return pl.pallas_call(
        kernel,
        out_shape=(
            jax.ShapeDtypeStruct((STEPS, cases, width), BF16),
            jax.ShapeDtypeStruct((2, HALF, cases, width), BF16),
        ),
        in_specs=[pl.BlockSpec(memory_space=pltpu.SMEM), whole, pl.BlockSpec(memory_space=pl.ANY)],
        out_specs=(whole, whole),
        scratch_shapes=[
            pltpu.VMEM((blocks_n,) + factor.shape[1:2] + factor.shape[3:], BF16),
            pltpu.VMEM((STEPS, cases, width), F32),
            pltpu.SemaphoreType.DMA((blocks_n,)),
        ],
        compiler_params=pltpu.CompilerParams(vmem_limit_bytes=(blocks_n // 2 + 8) * 2**20),
        cost_estimate=pl.CostEstimate(
            flops=2 * blocks_n * width * width * cases,
            bytes_accessed=cost * blocks_n * width * width * 2,
            transcendentals=0,
        ),
        name=name,
    )(place, rows, factor)


def origin_xor(bits, core):
    mask = 0
    if bits & 1:
        mask = jnp.where(core == 0, 1, 3)
    if bits & 2:
        mask = mask ^ jnp.where(core == 0, 3, 1)
    return mask


def outer_kernel(place_ref, *refs):
    forward_pieces = refs[0:CHIPS_Y]
    back_pieces = refs[CHIPS_Y : 2 * CHIPS_Y]
    factor_slots = (refs[2 * CHIPS_Y : 2 * CHIPS_Y + 2], refs[2 * CHIPS_Y + 2 : 2 * CHIPS_Y + 4])
    keep_ref, send_ref, factor, used, solved, factor_sem, used_sem, solved_sem = refs[2 * CHIPS_Y + 4 :]
    first, y, core, z, x = (place_ref[i] for i in range(5))
    rows_n = CHIPS_Y * CORES
    factor_copies = ([], [])
    for rb in range(CORES):
        for half in range(2):
            for low in range(8):
                slot = half * 8 + low
                near, far = origin_xor(slot & 3, core), origin_xor(slot >> 2, core)
                if rb == 0:
                    place = (z ^ far) * 4 + (x ^ near)
                else:
                    place = (z ^ near) * 4 + (x ^ far)
                copy = pltpu.make_async_copy(
                    factor_slots[rb][half].at[low], factor.at[rb, :, place], factor_sem.at[rb, slot]
                )
                copy.start()
                factor_copies[rb].append(copy)
    used_copies = ([], [])
    for rb in range(CORES):
        upper = CORES * y + rb < first
        for shift in range(CHIPS_Y):
            chip = lax.rem(y - shift + CHIPS_Y, CHIPS_Y)
            for side in range(CORES):
                place = chip * CORES + (side ^ core)
                target = used.at[rb, :, place]
                sem = used_sem.at[rb, shift, side]
                back = pltpu.make_async_copy(back_pieces[shift].at[side], target, sem)
                fore = pltpu.make_async_copy(forward_pieces[shift].at[side], target, sem)

                @pl.when(upper)
                def _(back=back):
                    back.start()

                @pl.when(jnp.logical_not(upper))
                def _(fore=fore):
                    fore.start()

                used_copies[rb].append(back)
    solved_copies = []
    for which in range(CORES):
        row = CORES * y + (core ^ which)
        rank = lax.rem(row - first + rows_n, rows_n)
        column = lax.rem(rank, HALF)
        for shift in range(CHIPS_Y):
            chip = lax.rem(y - shift + CHIPS_Y, CHIPS_Y)
            for side in range(CORES):
                place = chip * CORES + (side ^ core)
                copy = pltpu.make_async_copy(
                    back_pieces[shift].at[side, column], solved.at[which, place], solved_sem.at[which, shift, side]
                )
                copy.start()
                solved_copies.append(copy)
    for copies in factor_copies + used_copies:
        for copy in copies:
            copy.wait()
    for which, target in ((1, send_ref), (0, keep_ref)):
        rb = core ^ which
        total = None
        for k in range(HALF):
            left = factor[rb, k]
            right = used[rb, k]
            left = left.reshape(left.shape[0] * left.shape[1], left.shape[2])
            right = right.reshape(right.shape[0] * right.shape[1], right.shape[2])
            term = dot_nt(left, right)
            total = term if total is None else total + term
        target[0] = total
    for copy in solved_copies:
        copy.wait()
    for which, target in ((1, send_ref), (0, keep_ref)):
        panel = solved[which]
        panel = panel.reshape(panel.shape[0] * panel.shape[1], panel.shape[2])
        target[1] = jnp.transpose(panel.astype(F32))


def outer_product(place, forward_pieces, back_pieces, factor_slots):
    _, _, cases, width = forward_pieces[0].shape
    slices, slice_rows = 16, factor_slots[0].shape[2]
    all_cases = CHIPS_Y * CORES * cases
    out = jax.ShapeDtypeStruct((2, width, all_cases), F32)
    whole = pl.BlockSpec(memory_space=pltpu.VMEM)
    remote = pl.BlockSpec(memory_space=pl.ANY)
    return pl.pallas_call(
        outer_kernel,
        out_shape=(out, out),
        in_specs=[pl.BlockSpec(memory_space=pltpu.SMEM)] + [remote] * (2 * CHIPS_Y + 4),
        out_specs=(whole, whole),
        scratch_shapes=[
            pltpu.VMEM((CORES, HALF, slices, slice_rows, width), BF16),
            pltpu.VMEM((CORES, HALF, CHIPS_Y * CORES, cases, width), BF16),
            pltpu.VMEM((CORES, CHIPS_Y * CORES, cases, width), BF16),
            pltpu.SemaphoreType.DMA((CORES, slices)),
            pltpu.SemaphoreType.DMA((CORES, CHIPS_Y, CORES)),
            pltpu.SemaphoreType.DMA((CORES, CHIPS_Y, CORES)),
        ],
        compiler_params=pltpu.CompilerParams(vmem_limit_bytes=16 * 2**20),
        cost_estimate=pl.CostEstimate(
            flops=2 * CORES * HALF * width * width * all_cases,
            bytes_accessed=CORES * HALF * width * (width + all_cases) * 2,
            transcendentals=0,
        ),
        name="outer_product",
    )(place, *forward_pieces, *back_pieces, *factor_slots)


def finish_kernel(place_ref, kept_ref, got_ref, load_ref, out_ref):
    first, row, core = place_ref[0], place_ref[1] * CORES + place_ref[2], place_ref[2]
    rank = lax.rem(row - first + STEPS, STEPS)
    inside = lax.div(first + rank, STEPS)
    out_ref[1 - inside] = load_ref[...] - kept_ref[0] - got_ref[0]
    here = lax.div(rank, HALF) == core

    @pl.when(here)
    def _():
        out_ref[inside] = kept_ref[1]

    @pl.when(jnp.logical_not(here))
    def _():
        out_ref[inside] = got_ref[1]


def finish(place, kept, got, load):
    whole = pl.BlockSpec(memory_space=pltpu.VMEM)
    return pl.pallas_call(
        finish_kernel,
        out_shape=jax.ShapeDtypeStruct(kept.shape, F32),
        in_specs=[pl.BlockSpec(memory_space=pltpu.SMEM), whole, whole, whole],
        out_specs=whole,
        compiler_params=pltpu.CompilerParams(vmem_limit_bytes=8 * 2**20),
        name="finish",
    )(place, kept, got, load)


def device_pairs(move):
    pairs = []
    for y in range(4):
        for core in range(2):
            for z in range(4):
                for x in range(4):
                    to_y, to_core, to_z, to_x = move(y, core, z, x)
                    pairs.append(((y * 2 + core) * 16 + z * 4 + x, (to_y * 2 + to_core) * 16 + to_z * 4 + to_x))
    return pairs


def double(value, axis, step):
    masks = (1, 3) if step == 0 else (3, 1)

    def move(y, core, z, x):
        if axis == "x":
            return y, core, z, x ^ masks[core]
        return y, core, z ^ masks[core], x

    return lax.ppermute(value, ("row", "col"), device_pairs(move))


def swap_cores(value):
    return lax.ppermute(value, "row", [(r, r ^ 1) for r in range(CHIPS_Y * CORES)])


def round_y(value):
    rows = [(y, core) for y in range(CHIPS_Y) for core in range(CORES)]
    pieces = [value]
    for shift in range(1, CHIPS_Y):
        pairs = [(y * CORES + core, (y + shift) % CHIPS_Y * CORES + core) for y, core in rows]
        pieces.append(lax.ppermute(value, "row", pairs))
    return pieces


def own_half(kept, sent):
    return jnp.stack([kept, swap_cores(sent)])


def gather_outer_begin(slices, core):
    kept = lax.dynamic_slice_in_dim(slices, core * HALF, HALF, 0)
    sent = lax.dynamic_slice_in_dim(slices, (1 - core) * HALF, HALF, 0)
    both = own_half(kept, sent)
    first_row = jnp.where(core == 0, both[0], both[1])[None]
    second_row = jnp.where(core == 0, both[1], both[0])[None]
    parts = [first_row, second_row]
    for step in range(2):
        got = [double(part, "xz"[i], step) for i, part in enumerate(parts)]
        parts = [jnp.concatenate([part, new]) for part, new in zip(parts, got)]
    return parts


def gather_outer_round(parts, step):
    return [double(part, "zx"[i], step) for i, part in enumerate(parts)]


def shards(right_side, factor_store, col_owner, window_start, stress_kernel):
    rows_n = lax.axis_size("row")
    cols_n = lax.axis_size("col")
    row_id = lax.axis_index("row")
    col_id = lax.axis_index("col")
    core = row_id % CORES
    first = window_start[0]
    panels_dev, _, width, cases = right_side.shape
    own_cases = cases // rows_n
    slice_rows = width // cols_n
    rank = (row_id - first) % rows_n
    inside = (first + rank) // rows_n
    state = right_side.reshape(panels_dev, width, cases)
    factor = factor_store.reshape(panels_dev, width, width)

    ranks = jnp.arange(STEPS, dtype=jnp.int32)
    owners = jnp.take(col_owner, (first + ranks) % cols_n)

    def spread(panel):
        parts = panel.reshape(cols_n, slice_rows, width)
        parts = lax.all_to_all(parts, "col", 0, 0)
        return jnp.stack(
            [lax.dynamic_index_in_dim(parts, owners[k], 0, keepdims=False) for k in range(STEPS)]
        )

    window_factor = lax.dynamic_index_in_dim(factor, inside, 0, keepdims=False)
    outer_factor = lax.dynamic_index_in_dim(factor, 1 - inside, 0, keepdims=False)
    window_slices = spread(window_factor.T)
    gathered = lax.all_gather(window_slices, ("row", "col"))
    gathered = gathered.reshape(rows_n, cols_n, STEPS, slice_rows, width)

    outer_factor, state, window_slices = lax.optimization_barrier((outer_factor, state, window_slices))
    window_load = lax.dynamic_index_in_dim(state, inside, 0, keepdims=False)
    outer_load = lax.dynamic_index_in_dim(state, 1 - inside, 0, keepdims=False)
    load = window_load.T.reshape(rows_n, own_cases, width)
    load = lax.all_to_all(load, "row", 0, 0)
    outer_factor, load = lax.optimization_barrier((outer_factor, load))
    outer_parts = gather_outer_begin(spread(outer_factor), core)
    outer_parts, gathered, load = lax.optimization_barrier((outer_parts, gathered, load))
    place = jnp.stack([first, row_id // CORES, core, col_id // 4, col_id % 4]).astype(jnp.int32)
    outer_got = gather_outer_round(outer_parts, 0)
    forward, halves = substitution(forward_kernel, "forward", 28, 4, place, load, gathered)
    forward, halves, outer_parts, outer_got = lax.optimization_barrier((forward, halves, outer_parts, outer_got))
    forward_half = own_half(halves[0], halves[1])
    outer_parts = [jnp.concatenate([part, new]) for part, new in zip(outer_parts, outer_got)]
    forward, forward_half, outer_parts = lax.optimization_barrier((forward, forward_half, outer_parts))
    forward_pieces = round_y(forward_half)
    outer_got = gather_outer_round(outer_parts, 1)
    back, halves = substitution(backward_kernel, "backward", 36, 4, place, forward, gathered)
    back, halves, forward_pieces, outer_got = lax.optimization_barrier((back, halves, forward_pieces, outer_got))
    factor_slots = [outer_parts[0], outer_got[0], outer_parts[1], outer_got[1]]
    back_pieces = round_y(own_half(halves[0], halves[1]))

    stress = jnp.einsum("kcu,kus->cs", back, stress_kernel, preferred_element_type=F32)

    place, stress = lax.optimization_barrier((place, stress))
    kept, sent = outer_product(place, forward_pieces, back_pieces, factor_slots)
    result = finish(place, kept, swap_cores(sent), outer_load)
    return result.reshape(right_side.shape), stress


def solution(mesh):
    in_specs = (P(None, "row", None, "col"), P(None, "row", None, "col", None, None), P(), P(), P())
    out_specs = (P(None, "row", None, "col"), P(("col", "row"), None))
    return jax.shard_map(shards, mesh=mesh, in_specs=in_specs, out_specs=out_specs, check_vma=False)
```

```python
import jax
import jax.numpy as jnp
from jax import lax
from jax.experimental import pallas as pl
from jax.experimental.pallas import tpu as pltpu
from jax.sharding import PartitionSpec as P

STEPS = 8
HALF = STEPS // 2
CHIPS_Y = 4
CORES = 2
BF16 = jnp.bfloat16
F32 = jnp.float32


def dot_nn(a, b):
    return lax.dot_general(a, b, (((1,), (0,)), ((), ())), preferred_element_type=F32)


def dot_nt(a, b):
    return lax.dot_general(a, b, (((1,), (1,)), ((), ())), preferred_element_type=F32)


def solve_kernel(place_ref, load_ref, factor_ref, back_ref, halves_ref, *scratch):
    lower, upper, sems = scratch[: STEPS - 1], scratch[STEPS - 1 : -1], scratch[-1]
    first, core = place_ref[0], place_ref[2]
    lower_copies = [None]
    for p in range(1, STEPS):
        source = factor_ref.at[lax.rem(first + p, STEPS), :, 0:p]
        lower_copies.append(pltpu.make_async_copy(source, lower[p - 1], sems.at[p - 1]))
        lower_copies[p].start()
    upper_copies = [None] * STEPS
    for p in range(STEPS - 1, -1, -1):
        source = factor_ref.at[lax.rem(first + p, STEPS), :, p:STEPS]
        upper_copies[p] = pltpu.make_async_copy(source, upper[p], sems.at[STEPS - 1 + p])
        upper_copies[p].start()

    def block(ref, k):
        value = ref[:, k]
        return value.reshape(value.shape[0] * value.shape[1], value.shape[2])

    def solved(which, k, value):
        halves_ref[(k // HALF) ^ core, which, k % HALF] = value

    forward = []
    for p in range(STEPS):
        rows = load_ref[lax.rem(first + p, STEPS)]
        if p:
            lower_copies[p].wait()
        for k in range(p):
            rows = rows - dot_nn(forward[k], block(lower[p - 1], k))
        forward.append(rows.astype(BF16))
        solved(0, p, forward[p])
    back = [None] * STEPS
    for p in range(STEPS - 1, -1, -1):
        rows = forward[p].astype(F32)
        upper_copies[p].wait()
        for k in range(STEPS - 1, p, -1):
            rows = rows - dot_nn(back[k], block(upper[p], k - p))
        back[p] = dot_nn(rows.astype(BF16), block(upper[p], 0)).astype(BF16)
        back_ref[p] = back[p]
        solved(1, p, back[p])


def solve(place, load, factor):
    _, cases, width = load.shape
    _, slices, _, slice_rows, _ = factor.shape
    blocks_n = STEPS * STEPS
    whole = pl.BlockSpec(memory_space=pltpu.VMEM)
    return pl.pallas_call(
        solve_kernel,
        out_shape=(
            jax.ShapeDtypeStruct((STEPS, cases, width), BF16),
            jax.ShapeDtypeStruct((2, 2, HALF, cases, width), BF16),
        ),
        in_specs=[pl.BlockSpec(memory_space=pltpu.SMEM), whole, pl.BlockSpec(memory_space=pl.ANY)],
        out_specs=(whole, whole),
        scratch_shapes=[pltpu.VMEM((slices, p, slice_rows, width), BF16) for p in range(1, STEPS)]
        + [pltpu.VMEM((slices, STEPS - p, slice_rows, width), BF16) for p in range(STEPS)]
        + [pltpu.SemaphoreType.DMA((2 * STEPS - 1,))],
        compiler_params=pltpu.CompilerParams(vmem_limit_bytes=40 * 2**20),
        cost_estimate=pl.CostEstimate(
            flops=2 * blocks_n * width * width * cases,
            bytes_accessed=2 * blocks_n * width * width,
            transcendentals=0,
        ),
        name="solve",
    )(place, load, factor)


def origin_xor(bits, core):
    mask = 0
    if bits & 1:
        mask = jnp.where(core == 0, 1, 3)
    if bits & 2:
        mask = mask ^ jnp.where(core == 0, 3, 1)
    return mask


def outer_kernel(place_ref, *refs):
    pieces = refs[:CHIPS_Y]
    factor_slots = (refs[CHIPS_Y : CHIPS_Y + 2], refs[CHIPS_Y + 2 : CHIPS_Y + 4])
    keep_ref, send_ref, factor, used, factor_sem, used_sem = refs[CHIPS_Y + 4 :]
    first, y, core, z, x = (place_ref[i] for i in range(5))
    rows_n = CHIPS_Y * CORES
    copies = []
    for rb in range(CORES):
        for bits in range(4):
            far = origin_xor(bits, core)
            source = factor_slots[rb][bits >> 1].at[pl.ds((bits & 1) * 4, 4)]
            if rb == 0:
                target = factor.at[rb ^ core, z ^ far]
            else:
                target = factor.at[rb ^ core, :, x ^ far]
            copies.append(pltpu.make_async_copy(source, target, factor_sem.at[rb, bits]))
            copies[-1].start()
    for shift in range(CHIPS_Y):
        chip = lax.rem(y - shift + CHIPS_Y, CHIPS_Y)
        copies.append(pltpu.make_async_copy(pieces[shift], used.at[chip], used_sem.at[shift]))
        copies[-1].start()
    for copy in copies:
        copy.wait()

    def cases(kind, k):
        value = used[:, :, kind, k]
        return value.reshape(-1, value.shape[-1])

    for which, target in ((1, send_ref), (0, keep_ref)):
        row = CORES * y + (core ^ which)
        upper = (row < first).astype(jnp.int32)
        total = None
        for k in range(HALF):
            left = factor[which, :, :, k]
            term = dot_nt(left.reshape(-1, left.shape[-1]), cases(upper, k))
            total = term if total is None else total + term
        target[0] = total
        rank = lax.rem(row - first + rows_n, rows_n)
        target[1] = jnp.transpose(cases(1, lax.rem(rank, HALF)).astype(F32))


def outer_product(place, pieces, factor_slots):
    _, _, _, cases, width = pieces[0].shape
    slice_rows = factor_slots[0].shape[2]
    all_cases = CHIPS_Y * CORES * cases
    out = jax.ShapeDtypeStruct((2, width, all_cases), F32)
    whole = pl.BlockSpec(memory_space=pltpu.VMEM)
    remote = pl.BlockSpec(memory_space=pl.ANY)
    return pl.pallas_call(
        outer_kernel,
        out_shape=(out, out),
        in_specs=[pl.BlockSpec(memory_space=pltpu.SMEM)] + [remote] * (CHIPS_Y + 4),
        out_specs=(whole, whole),
        scratch_shapes=[
            pltpu.VMEM((CORES, 4, 4, HALF, slice_rows, width), BF16),
            pltpu.VMEM((CHIPS_Y,) + pieces[0].shape, BF16),
            pltpu.SemaphoreType.DMA((CORES, 4)),
            pltpu.SemaphoreType.DMA((CHIPS_Y,)),
        ],
        compiler_params=pltpu.CompilerParams(vmem_limit_bytes=16 * 2**20),
        cost_estimate=pl.CostEstimate(
            flops=2 * CORES * HALF * width * width * all_cases,
            bytes_accessed=CORES * HALF * width * (width + all_cases) * 2,
            transcendentals=0,
        ),
        name="outer_product",
    )(place, *pieces, *factor_slots)


def finish_kernel(place_ref, kept_ref, got_ref, load_ref, out_ref):
    first, row, core = place_ref[0], place_ref[1] * CORES + place_ref[2], place_ref[2]
    rank = lax.rem(row - first + STEPS, STEPS)
    inside = lax.div(first + rank, STEPS)
    out_ref[1 - inside] = load_ref[...] - kept_ref[0] - got_ref[0]
    here = lax.div(rank, HALF) == core

    @pl.when(here)
    def _():
        out_ref[inside] = kept_ref[1]

    @pl.when(jnp.logical_not(here))
    def _():
        out_ref[inside] = got_ref[1]


def finish(place, kept, got, load):
    whole = pl.BlockSpec(memory_space=pltpu.VMEM)
    return pl.pallas_call(
        finish_kernel,
        out_shape=jax.ShapeDtypeStruct(kept.shape, F32),
        in_specs=[pl.BlockSpec(memory_space=pltpu.SMEM), whole, whole, whole],
        out_specs=whole,
        compiler_params=pltpu.CompilerParams(vmem_limit_bytes=8 * 2**20),
        name="finish",
    )(place, kept, got, load)


def device_pairs(move):
    pairs = []
    for y in range(4):
        for core in range(2):
            for z in range(4):
                for x in range(4):
                    to_y, to_core, to_z, to_x = move(y, core, z, x)
                    pairs.append(((y * 2 + core) * 16 + z * 4 + x, (to_y * 2 + to_core) * 16 + to_z * 4 + to_x))
    return pairs


def double(value, axis, step):
    masks = (1, 3) if step == 0 else (3, 1)

    def move(y, core, z, x):
        if axis == "x":
            return y, core, z, x ^ masks[core]
        return y, core, z ^ masks[core], x

    return lax.ppermute(value, ("row", "col"), device_pairs(move))


def swap_cores(value):
    return lax.ppermute(value, "row", [(r, r ^ 1) for r in range(CHIPS_Y * CORES)])


def round_y(value):
    rows = [(y, core) for y in range(CHIPS_Y) for core in range(CORES)]
    pieces = [value]
    for shift in range(1, CHIPS_Y):
        pairs = [(y * CORES + core, (y + shift) % CHIPS_Y * CORES + core) for y, core in rows]
        pieces.append(lax.ppermute(value, "row", pairs))
    return pieces


def by_core(kept, sent, core):
    got = swap_cores(sent)
    return jnp.where(core == 0, kept, got), jnp.where(core == 0, got, kept)


def outer_slices(slices, core):
    kept = lax.dynamic_slice_in_dim(slices, core * HALF, HALF, 0)
    sent = lax.dynamic_slice_in_dim(slices, (1 - core) * HALF, HALF, 0)
    return [part[None] for part in by_core(kept, sent, core)]


def in_order(part, here, core):
    slots = []
    for coordinate in range(4):
        apart = coordinate ^ here
        slot = apart ^ (apart >> 1)
        slot = jnp.where(core == 0, slot, (slot & 1) * 2 + (slot >> 1))
        slots.append(lax.dynamic_index_in_dim(part, slot, 0, keepdims=False))
    return jnp.stack(slots)


def outer_round(parts, axes, step):
    return [double(part, axis, step) for part, axis in zip(parts, axes)]


def join(parts, got):
    return [jnp.concatenate([part, new]) for part, new in zip(parts, got)]


def shards(right_side, factor_store, col_owner, window_start, stress_kernel):
    rows_n = lax.axis_size("row")
    cols_n = lax.axis_size("col")
    row_id = lax.axis_index("row")
    col_id = lax.axis_index("col")
    core = row_id % CORES
    first = window_start[0]
    panels_dev, _, width, cases = right_side.shape
    own_cases = cases // rows_n
    slice_rows = width // cols_n
    rank = (row_id - first) % rows_n
    inside = (first + rank) // rows_n
    state = right_side.reshape(panels_dev, width, cases)
    factor = factor_store.reshape(panels_dev, width, width)

    ranks = jnp.arange(STEPS, dtype=jnp.int32)
    owners = jnp.take(col_owner, (first + ranks) % cols_n)

    def spread(panel):
        parts = panel.reshape(cols_n, slice_rows, width)
        parts = lax.all_to_all(parts, "col", 0, 0)
        return jnp.stack(
            [lax.dynamic_index_in_dim(parts, owners[k], 0, keepdims=False) for k in range(STEPS)]
        )

    window_factor = jnp.where(inside == 0, factor[0], factor[1])
    outer_factor = jnp.where(inside == 0, factor[1], factor[0])
    window_slices = spread(window_factor.T)
    gathered = lax.all_gather(window_slices, ("row", "col"))
    gathered = gathered.reshape(rows_n, cols_n, STEPS, slice_rows, width)

    outer_factor, state, window_slices = lax.optimization_barrier((outer_factor, state, window_slices))
    window_load = lax.dynamic_index_in_dim(state, inside, 0, keepdims=False)
    outer_load = lax.dynamic_index_in_dim(state, 1 - inside, 0, keepdims=False)
    load = window_load.T.reshape(rows_n, own_cases, width)
    load = lax.all_to_all(load, "row", 0, 0)
    outer_factor, load = lax.optimization_barrier((outer_factor, load))
    place = jnp.stack([first, row_id // CORES, core, col_id // 4, col_id % 4]).astype(jnp.int32)
    parts = outer_slices(spread(outer_factor), core)
    parts = join(parts, outer_round(parts, "xz", 0))
    parts = join(parts, outer_round(parts, "xz", 1))
    parts = [in_order(part, here, core) for part, here in zip(parts, (col_id % 4, col_id // 4))]
    parts = join(parts, outer_round(parts, "zx", 0))
    parts, gathered, load = lax.optimization_barrier((parts, gathered, load))
    back, halves = solve(place, load, gathered)
    both = jnp.stack(by_core(halves[0], halves[1], core))
    both, parts = lax.optimization_barrier((both, parts))
    pieces = round_y(both)
    got = outer_round(parts, "zx", 1)
    factor_slots = [parts[0], got[0], parts[1], got[1]]

    stress = jnp.einsum("kcu,kus->cs", back, stress_kernel, preferred_element_type=F32)

    place, stress = lax.optimization_barrier((place, stress))
    kept, sent = outer_product(place, pieces, factor_slots)
    result = finish(place, kept, swap_cores(sent), outer_load)
    return result.reshape(right_side.shape), stress


def solution(mesh):
    in_specs = (P(None, "row", None, "col"), P(None, "row", None, "col", None, None), P(), P(), P())
    out_specs = (P(None, "row", None, "col"), P(("col", "row"), None))
    return jax.shard_map(shards, mesh=mesh, in_specs=in_specs, out_specs=out_specs, check_vma=False)
```

```python
import jax
import jax.numpy as jnp
from jax import lax
from jax.experimental import pallas as pl
from jax.experimental.pallas import tpu as pltpu
from jax.sharding import PartitionSpec as P

STEPS = 8
HALF = STEPS // 2
CHIPS_Y = 4
CORES = 2
BF16 = jnp.bfloat16
F32 = jnp.float32


def dot_nn(a, b):
    return lax.dot_general(a, b, (((1,), (0,)), ((), ())), preferred_element_type=F32)


def dot_nt(a, b):
    return lax.dot_general(a, b, (((1,), (1,)), ((), ())), preferred_element_type=F32)


def solve_kernel(place_ref, load_ref, factor_ref, solved_ref, *scratch):
    lower, upper, sems = scratch[: STEPS - 1], scratch[STEPS - 1 : -1], scratch[-1]
    first = place_ref[0]
    lower_copies = [None]
    for p in range(1, STEPS):
        source = factor_ref.at[lax.rem(first + p, STEPS), :, 0:p]
        lower_copies.append(pltpu.make_async_copy(source, lower[p - 1], sems.at[p - 1]))
        lower_copies[p].start()
    upper_copies = [None] * STEPS
    for p in range(STEPS - 1, -1, -1):
        source = factor_ref.at[lax.rem(first + p, STEPS), :, p:STEPS]
        upper_copies[p] = pltpu.make_async_copy(source, upper[p], sems.at[STEPS - 1 + p])
        upper_copies[p].start()

    def block(ref, k):
        value = ref[:, k]
        return value.reshape(value.shape[0] * value.shape[1], value.shape[2])

    forward = []
    for p in range(STEPS):
        rows = load_ref[lax.rem(first + p, STEPS)]
        if p:
            lower_copies[p].wait()
        for k in range(p):
            rows = rows - dot_nn(forward[k], block(lower[p - 1], k))
        forward.append(rows.astype(BF16))
        solved_ref[0, p] = forward[p]
    back = [None] * STEPS
    for p in range(STEPS - 1, -1, -1):
        rows = forward[p].astype(F32)
        upper_copies[p].wait()
        for k in range(STEPS - 1, p, -1):
            rows = rows - dot_nn(back[k], block(upper[p], k - p))
        back[p] = dot_nn(rows.astype(BF16), block(upper[p], 0)).astype(BF16)
        solved_ref[1, p] = back[p]


def solve(place, load, factor):
    _, cases, width = load.shape
    _, slices, _, slice_rows, _ = factor.shape
    blocks_n = STEPS * STEPS
    whole = pl.BlockSpec(memory_space=pltpu.VMEM)
    return pl.pallas_call(
        solve_kernel,
        out_shape=jax.ShapeDtypeStruct((2, STEPS, cases, width), BF16),
        in_specs=[pl.BlockSpec(memory_space=pltpu.SMEM), whole, pl.BlockSpec(memory_space=pl.ANY)],
        out_specs=whole,
        scratch_shapes=[pltpu.VMEM((slices, p, slice_rows, width), BF16) for p in range(1, STEPS)]
        + [pltpu.VMEM((slices, STEPS - p, slice_rows, width), BF16) for p in range(STEPS)]
        + [pltpu.SemaphoreType.DMA((2 * STEPS - 1,))],
        compiler_params=pltpu.CompilerParams(vmem_limit_bytes=40 * 2**20),
        cost_estimate=pl.CostEstimate(
            flops=2 * blocks_n * width * width * cases,
            bytes_accessed=2 * blocks_n * width * width,
            transcendentals=0,
        ),
        name="solve",
    )(place, load, factor)


def origin_xor(bits, core):
    mask = 0
    if bits & 1:
        mask = jnp.where(core == 0, 1, 3)
    if bits & 2:
        mask = mask ^ jnp.where(core == 0, 3, 1)
    return mask


def outer_kernel(place_ref, state_ref, *refs):
    pieces = [refs[2 * chip : 2 * chip + 2] for chip in range(CHIPS_Y)]
    factor_slots = (refs[8:10], refs[10:12])
    out_ref, load, factor, used, solved, load_sem, factor_sem, used_sem, solved_sem = refs[12:]
    first, y, core, z, x = (place_ref[i] for i in range(5))
    row = CORES * y + core
    rank = lax.rem(row - first + STEPS, STEPS)
    inside = lax.div(first + rank, STEPS)
    upper = (row < first).astype(jnp.int32)
    copies = []

    def begin(source, target, sem):
        copies.append(pltpu.make_async_copy(source, target, sem))
        copies[-1].start()

    for half in range(2):
        for bits in range(4):
            far = origin_xor(bits, core)
            source = factor_slots[half][bits >> 1].at[pl.ds((bits & 1) * 4, 4)]
            target = factor.at[half, z ^ far] if half == 0 else factor.at[half, :, x ^ far]
            begin(source, target, factor_sem.at[half, bits])
    for shift in range(CHIPS_Y):
        chip = lax.rem(y - shift + CHIPS_Y, CHIPS_Y)
        for side in range(CORES):
            place = chip * CORES + (core ^ side)
            begin(pieces[shift][side].at[upper], used.at[place], used_sem.at[shift, side])
            begin(pieces[shift][side].at[1, rank], solved.at[place], solved_sem.at[shift, side])
    begin(state_ref.at[1 - inside], load, load_sem.at[0])
    for copy in copies:
        copy.wait()
    total = load[...]
    for half in range(2):
        for k in range(HALF):
            left = factor[half, :, :, k]
            right = used[:, half * HALF + k]
            total = total - dot_nt(left.reshape(-1, left.shape[-1]), right.reshape(-1, right.shape[-1]))
    out_ref[1 - inside] = total
    panel = solved[...]
    out_ref[inside] = jnp.transpose(panel.reshape(-1, panel.shape[-1]).astype(F32))


def outer_product(place, state, pieces, factor_slots):
    _, _, cases, width = pieces[0].shape
    slice_rows = factor_slots[0].shape[2]
    places = CHIPS_Y * CORES
    whole = pl.BlockSpec(memory_space=pltpu.VMEM)
    remote = pl.BlockSpec(memory_space=pl.ANY)
    return pl.pallas_call(
        outer_kernel,
        out_shape=jax.ShapeDtypeStruct(state.shape, F32),
        in_specs=[pl.BlockSpec(memory_space=pltpu.SMEM)] + [remote] * (1 + 2 * CHIPS_Y + 4),
        out_specs=whole,
        scratch_shapes=[
            pltpu.VMEM(state.shape[1:], F32),
            pltpu.VMEM((2, 4, 4, HALF, slice_rows, width), BF16),
            pltpu.VMEM((places, STEPS, cases, width), BF16),
            pltpu.VMEM((places, cases, width), BF16),
            pltpu.SemaphoreType.DMA((1,)),
            pltpu.SemaphoreType.DMA((2, 4)),
            pltpu.SemaphoreType.DMA((CHIPS_Y, CORES)),
            pltpu.SemaphoreType.DMA((CHIPS_Y, CORES)),
        ],
        compiler_params=pltpu.CompilerParams(vmem_limit_bytes=16 * 2**20),
        cost_estimate=pl.CostEstimate(
            flops=2 * STEPS * width * width * places * cases,
            bytes_accessed=2 * STEPS * width * (width + places * cases),
            transcendentals=0,
        ),
        name="outer_product",
    )(place, state, *pieces, *factor_slots)


def device_pairs(move):
    pairs = []
    for y in range(4):
        for core in range(2):
            for z in range(4):
                for x in range(4):
                    to_y, to_core, to_z, to_x = move(y, core, z, x)
                    pairs.append(((y * 2 + core) * 16 + z * 4 + x, (to_y * 2 + to_core) * 16 + to_z * 4 + to_x))
    return pairs


def double(value, axis, step):
    masks = (1, 3) if step == 0 else (3, 1)

    def move(y, core, z, x):
        if axis == "x":
            return y, core, z, x ^ masks[core]
        return y, core, z ^ masks[core], x

    return lax.ppermute(value, ("row", "col"), device_pairs(move))


def swap_cores(value):
    return lax.ppermute(value, "row", [(r, r ^ 1) for r in range(CHIPS_Y * CORES)])


def round_y(value):
    rows = [(y, core) for y in range(CHIPS_Y) for core in range(CORES)]
    pieces = [value]
    for shift in range(1, CHIPS_Y):
        pairs = [(y * CORES + core, (y + shift) % CHIPS_Y * CORES + core) for y, core in rows]
        pieces.append(lax.ppermute(value, "row", pairs))
    return pieces


def in_order(part, here, core):
    slots = []
    for coordinate in range(4):
        apart = coordinate ^ here
        slot = apart ^ (apart >> 1)
        slot = jnp.where(core == 0, slot, (slot & 1) * 2 + (slot >> 1))
        slots.append(lax.dynamic_index_in_dim(part, slot, 0, keepdims=False))
    return jnp.stack(slots)


def outer_round(parts, axes, step):
    return [double(part, axis, step) for part, axis in zip(parts, axes)]


def join(parts, got):
    return [jnp.concatenate([part, new]) for part, new in zip(parts, got)]


def shards(right_side, factor_store, col_owner, window_start, stress_kernel):
    rows_n = lax.axis_size("row")
    cols_n = lax.axis_size("col")
    row_id = lax.axis_index("row")
    col_id = lax.axis_index("col")
    core = row_id % CORES
    first = window_start[0]
    panels_dev, _, width, cases = right_side.shape
    own_cases = cases // rows_n
    slice_rows = width // cols_n
    rank = (row_id - first) % rows_n
    inside = (first + rank) // rows_n
    state = right_side.reshape(panels_dev, width, cases)
    factor = factor_store.reshape(panels_dev, width, width)

    ranks = jnp.arange(STEPS, dtype=jnp.int32)
    owners = jnp.take(col_owner, (first + ranks) % cols_n)

    def spread(panel):
        parts = panel.reshape(cols_n, slice_rows, width)
        parts = lax.all_to_all(parts, "col", 0, 0)
        return jnp.stack(
            [lax.dynamic_index_in_dim(parts, owners[k], 0, keepdims=False) for k in range(STEPS)]
        )

    window_factor = jnp.where(inside == 0, factor[0], factor[1])
    outer_factor = jnp.where(inside == 0, factor[1], factor[0])
    window_slices = spread(window_factor.T)
    gathered = lax.all_gather(window_slices, ("row", "col"))
    gathered = gathered.reshape(rows_n, cols_n, STEPS, slice_rows, width)

    outer_factor, state, window_slices = lax.optimization_barrier((outer_factor, state, window_slices))
    window_load = lax.dynamic_index_in_dim(state, inside, 0, keepdims=False)
    load = window_load.T.reshape(rows_n, own_cases, width)
    load = lax.all_to_all(load, "row", 0, 0)
    outer_factor, load = lax.optimization_barrier((outer_factor, load))
    place = jnp.stack([first, row_id // CORES, core, col_id // 4, col_id % 4]).astype(jnp.int32)
    slices = spread(outer_factor)
    parts = [slices[None, :HALF], slices[None, HALF:]]
    parts = join(parts, outer_round(parts, "xz", 0))
    parts = join(parts, outer_round(parts, "xz", 1))
    parts = [in_order(part, here, core) for part, here in zip(parts, (col_id % 4, col_id // 4))]
    parts = join(parts, outer_round(parts, "zx", 0))
    parts, gathered, load = lax.optimization_barrier((parts, gathered, load))
    solved = solve(place, load, gathered)
    stress = jnp.einsum("kcu,kus->cs", solved[1], stress_kernel, preferred_element_type=F32)
    arrived = round_y(solved)
    arrived[0], stress = lax.optimization_barrier((arrived[0], stress))
    pieces = []
    for piece in arrived:
        pieces += [piece, swap_cores(piece)]
    parts, solved = lax.optimization_barrier((parts, solved))
    got = outer_round(parts, "zx", 1)
    factor_slots = [parts[0], got[0], parts[1], got[1]]

    result = outer_product(place, state, pieces, factor_slots)
    return result.reshape(right_side.shape), stress


def solution(mesh):
    in_specs = (P(None, "row", None, "col"), P(None, "row", None, "col", None, None), P(), P(), P())
    out_specs = (P(None, "row", None, "col"), P(("col", "row"), None))
    return jax.shard_map(shards, mesh=mesh, in_specs=in_specs, out_specs=out_specs, check_vma=False)
```

```python
import jax
import jax.numpy as jnp
from jax import lax
from jax.experimental import pallas as pl
from jax.experimental.pallas import tpu as pltpu
from jax.sharding import PartitionSpec as P

STEPS = 8
HALF = STEPS // 2
CHIPS_Y = 4
CORES = 2
BF16 = jnp.bfloat16
F32 = jnp.float32


def dot_nn(a, b):
    return lax.dot_general(a, b, (((1,), (0,)), ((), ())), preferred_element_type=F32)


def dot_nt(a, b):
    return lax.dot_general(a, b, (((1,), (1,)), ((), ())), preferred_element_type=F32)


def solve_kernel(place_ref, load_ref, factor_ref, solved_ref, *scratch):
    lower, upper, sems = scratch[: STEPS - 1], scratch[STEPS - 1 : -1], scratch[-1]
    first = place_ref[0]
    lower_copies = [None]
    for p in range(1, STEPS):
        source = factor_ref.at[lax.rem(first + p, STEPS), :, 0:p]
        lower_copies.append(pltpu.make_async_copy(source, lower[p - 1], sems.at[p - 1]))
        lower_copies[p].start()
    upper_copies = [None] * STEPS
    for p in range(STEPS - 1, -1, -1):
        source = factor_ref.at[lax.rem(first + p, STEPS), :, p:STEPS]
        upper_copies[p] = pltpu.make_async_copy(source, upper[p], sems.at[STEPS - 1 + p])
        upper_copies[p].start()

    def block(ref, k):
        value = ref[:, k]
        return value.reshape(value.shape[0] * value.shape[1], value.shape[2])

    forward = []
    for p in range(STEPS):
        rows = load_ref[lax.rem(first + p, STEPS)]
        if p:
            lower_copies[p].wait()
        for k in range(p):
            rows = rows - dot_nn(forward[k], block(lower[p - 1], k))
        forward.append(rows.astype(BF16))
        solved_ref[0, p] = forward[p]
    back = [None] * STEPS
    for p in range(STEPS - 1, -1, -1):
        rows = forward[p].astype(F32)
        upper_copies[p].wait()
        for k in range(STEPS - 1, p, -1):
            rows = rows - dot_nn(back[k], block(upper[p], k - p))
        back[p] = dot_nn(rows.astype(BF16), block(upper[p], 0)).astype(BF16)
        solved_ref[1, p] = back[p]


def solve(place, load, factor):
    _, cases, width = load.shape
    _, slices, _, slice_rows, _ = factor.shape
    blocks_n = STEPS * STEPS
    whole = pl.BlockSpec(memory_space=pltpu.VMEM)
    return pl.pallas_call(
        solve_kernel,
        out_shape=jax.ShapeDtypeStruct((2, STEPS, cases, width), BF16),
        in_specs=[pl.BlockSpec(memory_space=pltpu.SMEM), whole, pl.BlockSpec(memory_space=pl.ANY)],
        out_specs=whole,
        scratch_shapes=[pltpu.VMEM((slices, p, slice_rows, width), BF16) for p in range(1, STEPS)]
        + [pltpu.VMEM((slices, STEPS - p, slice_rows, width), BF16) for p in range(STEPS)]
        + [pltpu.SemaphoreType.DMA((2 * STEPS - 1,))],
        compiler_params=pltpu.CompilerParams(vmem_limit_bytes=40 * 2**20),
        cost_estimate=pl.CostEstimate(
            flops=2 * blocks_n * width * width * cases,
            bytes_accessed=2 * blocks_n * width * width,
            transcendentals=0,
        ),
        name="solve",
    )(place, load, factor)


def origin_xor(bits, core):
    mask = 0
    if bits & 1:
        mask = jnp.where(core == 0, 1, 3)
    if bits & 2:
        mask = mask ^ jnp.where(core == 0, 3, 1)
    return mask


def outer_kernel(place_ref, state_ref, *refs):
    pieces = [refs[2 * chip : 2 * chip + 2] for chip in range(CHIPS_Y)]
    factor_slots = (refs[8:10], refs[10:12])
    out_ref, load, factor, used, solved, load_sem, factor_sem, used_sem, solved_sem = refs[12:]
    first, y, core, z, x = (place_ref[i] for i in range(5))
    row = CORES * y + core
    rank = lax.rem(row - first + STEPS, STEPS)
    inside = lax.div(first + rank, STEPS)
    upper = (row < first).astype(jnp.int32)
    copies = []

    def begin(source, target, sem):
        copies.append(pltpu.make_async_copy(source, target, sem))
        copies[-1].start()

    for half in range(2):
        for bits in range(4):
            far = origin_xor(bits, core)
            source = factor_slots[half][bits >> 1].at[pl.ds((bits & 1) * 4, 4)]
            target = factor.at[half, z ^ far] if half == 0 else factor.at[half, :, x ^ far]
            begin(source, target, factor_sem.at[half, bits])
    for shift in range(CHIPS_Y):
        chip = lax.rem(y - shift + CHIPS_Y, CHIPS_Y)
        for side in range(CORES):
            place = chip * CORES + (core ^ side)
            begin(pieces[shift][side].at[upper], used.at[place], used_sem.at[shift, side])
            begin(pieces[shift][side].at[1, rank], solved.at[place], solved_sem.at[shift, side])
    begin(state_ref.at[1 - inside], load, load_sem.at[0])
    for copy in copies:
        copy.wait()
    total = load[...]
    for half in range(2):
        for k in range(HALF):
            left = factor[half, :, :, k]
            right = used[:, half * HALF + k]
            total = total - dot_nt(left.reshape(-1, left.shape[-1]), right.reshape(-1, right.shape[-1]))
    out_ref[1 - inside] = total
    panel = solved[...]
    out_ref[inside] = jnp.transpose(panel.reshape(-1, panel.shape[-1]).astype(F32))


def outer_product(place, state, pieces, factor_slots):
    _, _, cases, width = pieces[0].shape
    slice_rows = factor_slots[0].shape[2]
    places = CHIPS_Y * CORES
    whole = pl.BlockSpec(memory_space=pltpu.VMEM)
    remote = pl.BlockSpec(memory_space=pl.ANY)
    return pl.pallas_call(
        outer_kernel,
        out_shape=jax.ShapeDtypeStruct(state.shape, F32),
        in_specs=[pl.BlockSpec(memory_space=pltpu.SMEM)] + [remote] * (1 + 2 * CHIPS_Y + 4),
        out_specs=whole,
        scratch_shapes=[
            pltpu.VMEM(state.shape[1:], F32),
            pltpu.VMEM((2, 4, 4, HALF, slice_rows, width), BF16),
            pltpu.VMEM((places, STEPS, cases, width), BF16),
            pltpu.VMEM((places, cases, width), BF16),
            pltpu.SemaphoreType.DMA((1,)),
            pltpu.SemaphoreType.DMA((2, 4)),
            pltpu.SemaphoreType.DMA((CHIPS_Y, CORES)),
            pltpu.SemaphoreType.DMA((CHIPS_Y, CORES)),
        ],
        compiler_params=pltpu.CompilerParams(vmem_limit_bytes=16 * 2**20),
        cost_estimate=pl.CostEstimate(
            flops=2 * STEPS * width * width * places * cases,
            bytes_accessed=2 * STEPS * width * (width + places * cases),
            transcendentals=0,
        ),
        name="outer_product",
    )(place, state, *pieces, *factor_slots)


def pick_kernel(start_ref, owner_ref, parts_ref, out_ref, sems):
    copies = []
    for k in range(STEPS):
        owner = owner_ref[lax.rem(start_ref[0] + k, parts_ref.shape[0])]
        copies.append(pltpu.make_async_copy(parts_ref.at[owner], out_ref.at[k], sems.at[k]))
        copies[k].start()
    for copy in copies:
        copy.wait()


def pick_columns(window_start, col_owner, parts):
    scalars = pl.BlockSpec(memory_space=pltpu.SMEM)
    return pl.pallas_call(
        pick_kernel,
        out_shape=jax.ShapeDtypeStruct((STEPS,) + parts.shape[1:], parts.dtype),
        in_specs=[scalars, scalars, pl.BlockSpec(memory_space=pl.ANY)],
        out_specs=pl.BlockSpec(memory_space=pltpu.VMEM),
        scratch_shapes=[pltpu.SemaphoreType.DMA((STEPS,))],
        cost_estimate=pl.CostEstimate(flops=0, bytes_accessed=64 * parts.size, transcendentals=0),
        name="pick_columns",
    )(window_start, col_owner, parts)


def device_pairs(move):
    pairs = []
    for y in range(4):
        for core in range(2):
            for z in range(4):
                for x in range(4):
                    to_y, to_core, to_z, to_x = move(y, core, z, x)
                    pairs.append(((y * 2 + core) * 16 + z * 4 + x, (to_y * 2 + to_core) * 16 + to_z * 4 + to_x))
    return pairs


def double(value, axis, step):
    masks = (1, 3) if step == 0 else (3, 1)

    def move(y, core, z, x):
        if axis == "x":
            return y, core, z, x ^ masks[core]
        return y, core, z ^ masks[core], x

    return lax.ppermute(value, ("row", "col"), device_pairs(move))


def swap_cores(value):
    return lax.ppermute(value, "row", [(r, r ^ 1) for r in range(CHIPS_Y * CORES)])


def round_y(value):
    rows = [(y, core) for y in range(CHIPS_Y) for core in range(CORES)]
    pieces = [value]
    for shift in range(1, CHIPS_Y):
        pairs = [(y * CORES + core, (y + shift) % CHIPS_Y * CORES + core) for y, core in rows]
        pieces.append(lax.ppermute(value, "row", pairs))
    return pieces


def in_order(part, here, core):
    slots = []
    for coordinate in range(4):
        apart = coordinate ^ here
        slot = apart ^ (apart >> 1)
        slot = jnp.where(core == 0, slot, (slot & 1) * 2 + (slot >> 1))
        slots.append(lax.dynamic_index_in_dim(part, slot, 0, keepdims=False))
    return jnp.stack(slots)


def outer_round(parts, axes, step):
    return [double(part, axis, step) for part, axis in zip(parts, axes)]


def join(parts, got):
    return [jnp.concatenate([part, new]) for part, new in zip(parts, got)]


def shards(right_side, factor_store, col_owner, window_start, stress_kernel):
    rows_n = lax.axis_size("row")
    cols_n = lax.axis_size("col")
    row_id = lax.axis_index("row")
    col_id = lax.axis_index("col")
    core = row_id % CORES
    first = window_start[0]
    panels_dev, _, width, cases = right_side.shape
    own_cases = cases // rows_n
    slice_rows = width // cols_n
    rank = (row_id - first) % rows_n
    inside = (first + rank) // rows_n
    state = right_side.reshape(panels_dev, width, cases)
    factor = factor_store.reshape(panels_dev, width, width)

    def spread(panel):
        parts = lax.all_to_all(panel.reshape(cols_n, slice_rows, width), "col", 0, 0)
        return pick_columns(window_start, col_owner, parts)

    window_factor = jnp.where(inside == 0, factor[0], factor[1])
    outer_factor = jnp.where(inside == 0, factor[1], factor[0])
    window_slices = spread(window_factor.T)
    gathered = lax.all_gather(window_slices, ("row", "col"))
    gathered = gathered.reshape(rows_n, cols_n, STEPS, slice_rows, width)

    outer_factor, state, window_slices = lax.optimization_barrier((outer_factor, state, window_slices))
    window_load = lax.dynamic_index_in_dim(state, inside, 0, keepdims=False)
    load = window_load.T.reshape(rows_n, own_cases, width)
    load = lax.all_to_all(load, "row", 0, 0)
    outer_factor, load = lax.optimization_barrier((outer_factor, load))
    place = jnp.stack([first, row_id // CORES, core, col_id // 4, col_id % 4]).astype(jnp.int32)
    slices = spread(outer_factor)
    parts = [slices[None, :HALF], slices[None, HALF:]]
    parts = join(parts, outer_round(parts, "xz", 0))
    parts = join(parts, outer_round(parts, "xz", 1))
    parts = [in_order(part, here, core) for part, here in zip(parts, (col_id % 4, col_id // 4))]
    parts = join(parts, outer_round(parts, "zx", 0))
    parts, gathered, load = lax.optimization_barrier((parts, gathered, load))
    solved = solve(place, load, gathered)
    stress = jnp.einsum("kcu,kus->cs", solved[1], stress_kernel, preferred_element_type=F32)
    arrived = round_y(solved)
    arrived[0], stress = lax.optimization_barrier((arrived[0], stress))
    pieces = []
    for piece in arrived:
        pieces += [piece, swap_cores(piece)]
    parts, solved = lax.optimization_barrier((parts, solved))
    got = outer_round(parts, "zx", 1)
    factor_slots = [parts[0], got[0], parts[1], got[1]]

    result = outer_product(place, state, pieces, factor_slots)
    return result.reshape(right_side.shape), stress


def solution(mesh):
    in_specs = (P(None, "row", None, "col"), P(None, "row", None, "col", None, None), P(), P(), P())
    out_specs = (P(None, "row", None, "col"), P(("col", "row"), None))
    return jax.shard_map(shards, mesh=mesh, in_specs=in_specs, out_specs=out_specs, check_vma=False)
```

```python
import jax
import jax.numpy as jnp
from jax import lax
from jax.experimental import pallas as pl
from jax.experimental.pallas import tpu as pltpu
from jax.sharding import PartitionSpec as P

STEPS = 8
HALF = STEPS // 2
CHIPS_Y = 4
CORES = 2
BF16 = jnp.bfloat16
F32 = jnp.float32


def dot_nn(a, b):
    return lax.dot_general(a, b, (((1,), (0,)), ((), ())), preferred_element_type=F32)


def dot_nt(a, b):
    return lax.dot_general(a, b, (((1,), (1,)), ((), ())), preferred_element_type=F32)


def solve_kernel(place_ref, load_ref, factor_ref, solved_ref, *scratch):
    lower, upper, sems = scratch[: STEPS - 1], scratch[STEPS - 1 : -1], scratch[-1]
    first = place_ref[0]
    lower_copies = [None]
    for p in range(1, STEPS):
        source = factor_ref.at[lax.rem(first + p, STEPS), :, 0:p]
        lower_copies.append(pltpu.make_async_copy(source, lower[p - 1], sems.at[p - 1]))
        lower_copies[p].start()
    upper_copies = [None] * STEPS
    for p in range(STEPS - 1, -1, -1):
        source = factor_ref.at[lax.rem(first + p, STEPS), :, p:STEPS]
        upper_copies[p] = pltpu.make_async_copy(source, upper[p], sems.at[STEPS - 1 + p])
        upper_copies[p].start()

    def block(ref, k):
        value = ref[:, k]
        return value.reshape(value.shape[0] * value.shape[1], value.shape[2])

    forward = []
    for p in range(STEPS):
        rows = load_ref[lax.rem(first + p, STEPS)]
        if p:
            lower_copies[p].wait()
        for k in range(p):
            rows = rows - dot_nn(forward[k], block(lower[p - 1], k))
        forward.append(rows.astype(BF16))
        solved_ref[0, p] = forward[p]
    back = [None] * STEPS
    for p in range(STEPS - 1, -1, -1):
        rows = forward[p].astype(F32)
        upper_copies[p].wait()
        for k in range(STEPS - 1, p, -1):
            rows = rows - dot_nn(back[k], block(upper[p], k - p))
        back[p] = dot_nn(rows.astype(BF16), block(upper[p], 0)).astype(BF16)
        solved_ref[1, p] = back[p]


def solve(place, load, factor):
    _, cases, width = load.shape
    _, slices, _, slice_rows, _ = factor.shape
    blocks_n = STEPS * STEPS
    whole = pl.BlockSpec(memory_space=pltpu.VMEM)
    return pl.pallas_call(
        solve_kernel,
        out_shape=jax.ShapeDtypeStruct((2, STEPS, cases, width), BF16),
        in_specs=[pl.BlockSpec(memory_space=pltpu.SMEM), whole, pl.BlockSpec(memory_space=pl.ANY)],
        out_specs=whole,
        scratch_shapes=[pltpu.VMEM((slices, p, slice_rows, width), BF16) for p in range(1, STEPS)]
        + [pltpu.VMEM((slices, STEPS - p, slice_rows, width), BF16) for p in range(STEPS)]
        + [pltpu.SemaphoreType.DMA((2 * STEPS - 1,))],
        compiler_params=pltpu.CompilerParams(vmem_limit_bytes=40 * 2**20),
        cost_estimate=pl.CostEstimate(
            flops=2 * blocks_n * width * width * cases,
            bytes_accessed=2 * blocks_n * width * width,
            transcendentals=0,
        ),
        name="solve",
    )(place, load, factor)


def origin_xor(bits, core):
    mask = 0
    if bits & 1:
        mask = jnp.where(core == 0, 1, 3)
    if bits & 2:
        mask = mask ^ jnp.where(core == 0, 3, 1)
    return mask


def outer_kernel(place_ref, state_ref, *refs):
    pieces = [refs[2 * chip : 2 * chip + 2] for chip in range(CHIPS_Y)]
    factor_slots = (refs[8:10], refs[10:12])
    out_ref, load, factor, used, solved, load_sem, factor_sem, used_sem, solved_sem = refs[12:]
    first, y, core, z, x = (place_ref[i] for i in range(5))
    row = CORES * y + core
    rank = lax.rem(row - first + STEPS, STEPS)
    inside = lax.div(first + rank, STEPS)
    upper = (row < first).astype(jnp.int32)

    def begin(source, target, sem):
        copy = pltpu.make_async_copy(source, target, sem)
        copy.start()
        return copy

    solved_copies, used_copies, factor_copies = [], [], ([], [])
    for shift in range(CHIPS_Y):
        chip = lax.rem(y - shift + CHIPS_Y, CHIPS_Y)
        for side in range(CORES):
            place = chip * CORES + (core ^ side)
            piece = pieces[shift][side]
            solved_copies.append(begin(piece.at[1, rank], solved.at[place], solved_sem.at[shift, side]))
            used_copies.append(begin(piece.at[upper], used.at[place], used_sem.at[shift, side]))
    used_copies.append(begin(state_ref.at[1 - inside], load, load_sem.at[0]))
    for half in range(2):
        for bits in range(4):
            far = origin_xor(bits, core)
            source = factor_slots[half][bits >> 1].at[pl.ds((bits & 1) * 4, 4)]
            target = factor.at[half, z ^ far] if half == 0 else factor.at[half, :, x ^ far]
            factor_copies[half].append(begin(source, target, factor_sem.at[half, bits]))
    for copy in solved_copies:
        copy.wait()
    panel = solved[...]
    out_ref[inside] = jnp.transpose(panel.reshape(-1, panel.shape[-1]).astype(F32))
    for copy in used_copies:
        copy.wait()
    total = load[...]
    for half in range(2):
        for copy in factor_copies[half]:
            copy.wait()
        for k in range(HALF):
            left = factor[half, :, :, k]
            right = used[:, half * HALF + k]
            total = total - dot_nt(left.reshape(-1, left.shape[-1]), right.reshape(-1, right.shape[-1]))
    out_ref[1 - inside] = total


def outer_product(place, state, pieces, factor_slots):
    _, _, cases, width = pieces[0].shape
    slice_rows = factor_slots[0].shape[2]
    places = CHIPS_Y * CORES
    whole = pl.BlockSpec(memory_space=pltpu.VMEM)
    remote = pl.BlockSpec(memory_space=pl.ANY)
    return pl.pallas_call(
        outer_kernel,
        out_shape=jax.ShapeDtypeStruct(state.shape, F32),
        in_specs=[pl.BlockSpec(memory_space=pltpu.SMEM)] + [remote] * (1 + 2 * CHIPS_Y + 4),
        out_specs=whole,
        scratch_shapes=[
            pltpu.VMEM(state.shape[1:], F32),
            pltpu.VMEM((2, 4, 4, HALF, slice_rows, width), BF16),
            pltpu.VMEM((places, STEPS, cases, width), BF16),
            pltpu.VMEM((places, cases, width), BF16),
            pltpu.SemaphoreType.DMA((1,)),
            pltpu.SemaphoreType.DMA((2, 4)),
            pltpu.SemaphoreType.DMA((CHIPS_Y, CORES)),
            pltpu.SemaphoreType.DMA((CHIPS_Y, CORES)),
        ],
        compiler_params=pltpu.CompilerParams(vmem_limit_bytes=16 * 2**20),
        cost_estimate=pl.CostEstimate(
            flops=2 * STEPS * width * width * places * cases,
            bytes_accessed=2 * STEPS * width * (width + places * cases),
            transcendentals=0,
        ),
        name="outer_product",
    )(place, state, *pieces, *factor_slots)


def pick_kernel(start_ref, owner_ref, parts_ref, out_ref, sems):
    copies = []
    for k in range(STEPS):
        owner = owner_ref[lax.rem(start_ref[0] + k, parts_ref.shape[0])]
        copies.append(pltpu.make_async_copy(parts_ref.at[owner], out_ref.at[k], sems.at[k]))
        copies[k].start()
    for copy in copies:
        copy.wait()


def pick_columns(window_start, col_owner, parts):
    scalars = pl.BlockSpec(memory_space=pltpu.SMEM)
    return pl.pallas_call(
        pick_kernel,
        out_shape=jax.ShapeDtypeStruct((STEPS,) + parts.shape[1:], parts.dtype),
        in_specs=[scalars, scalars, pl.BlockSpec(memory_space=pl.ANY)],
        out_specs=pl.BlockSpec(memory_space=pltpu.VMEM),
        scratch_shapes=[pltpu.SemaphoreType.DMA((STEPS,))],
        cost_estimate=pl.CostEstimate(flops=0, bytes_accessed=64 * parts.size, transcendentals=0),
        name="pick_columns",
    )(window_start, col_owner, parts)


def device_pairs(move):
    pairs = []
    for y in range(4):
        for core in range(2):
            for z in range(4):
                for x in range(4):
                    to_y, to_core, to_z, to_x = move(y, core, z, x)
                    pairs.append(((y * 2 + core) * 16 + z * 4 + x, (to_y * 2 + to_core) * 16 + to_z * 4 + to_x))
    return pairs


def double(value, axis, step):
    masks = (1, 3) if step == 0 else (3, 1)

    def move(y, core, z, x):
        if axis == "x":
            return y, core, z, x ^ masks[core]
        return y, core, z ^ masks[core], x

    return lax.ppermute(value, ("row", "col"), device_pairs(move))


def swap_cores(value):
    return lax.ppermute(value, "row", [(r, r ^ 1) for r in range(CHIPS_Y * CORES)])


def round_y(value):
    rows = [(y, core) for y in range(CHIPS_Y) for core in range(CORES)]
    pieces = [value]
    for shift in range(1, CHIPS_Y):
        pairs = [(y * CORES + core, (y + shift) % CHIPS_Y * CORES + core) for y, core in rows]
        pieces.append(lax.ppermute(value, "row", pairs))
    return pieces


def in_order(part, here, core):
    slots = []
    for coordinate in range(4):
        apart = coordinate ^ here
        slot = apart ^ (apart >> 1)
        slot = jnp.where(core == 0, slot, (slot & 1) * 2 + (slot >> 1))
        slots.append(lax.dynamic_index_in_dim(part, slot, 0, keepdims=False))
    return jnp.stack(slots)


def outer_round(parts, axes, step):
    return [double(part, axis, step) for part, axis in zip(parts, axes)]


def join(parts, got):
    return [jnp.concatenate([part, new]) for part, new in zip(parts, got)]


def shards(right_side, factor_store, col_owner, window_start, stress_kernel):
    rows_n = lax.axis_size("row")
    cols_n = lax.axis_size("col")
    row_id = lax.axis_index("row")
    col_id = lax.axis_index("col")
    core = row_id % CORES
    first = window_start[0]
    panels_dev, _, width, cases = right_side.shape
    own_cases = cases // rows_n
    slice_rows = width // cols_n
    rank = (row_id - first) % rows_n
    inside = (first + rank) // rows_n
    state = right_side.reshape(panels_dev, width, cases)
    factor = factor_store.reshape(panels_dev, width, width)

    def spread(panel):
        parts = lax.all_to_all(panel.reshape(cols_n, slice_rows, width), "col", 0, 0)
        return pick_columns(window_start, col_owner, parts)

    window_factor = jnp.where(inside == 0, factor[0], factor[1])
    outer_factor = jnp.where(inside == 0, factor[1], factor[0])
    window_slices = spread(window_factor.T)
    gathered = lax.all_gather(window_slices, ("row", "col"))
    gathered = gathered.reshape(rows_n, cols_n, STEPS, slice_rows, width)

    outer_factor, state, window_slices = lax.optimization_barrier((outer_factor, state, window_slices))
    window_load = lax.dynamic_index_in_dim(state, inside, 0, keepdims=False)
    load = window_load.T.reshape(rows_n, own_cases, width)
    load = lax.all_to_all(load, "row", 0, 0)
    outer_factor, load = lax.optimization_barrier((outer_factor, load))
    place = jnp.stack([first, row_id // CORES, core, col_id // 4, col_id % 4]).astype(jnp.int32)
    slices = spread(outer_factor)
    parts = [slices[None, :HALF], slices[None, HALF:]]
    parts = join(parts, outer_round(parts, "xz", 0))
    parts = join(parts, outer_round(parts, "xz", 1))
    parts = [in_order(part, here, core) for part, here in zip(parts, (col_id % 4, col_id // 4))]
    parts, gathered, load = lax.optimization_barrier((parts, gathered, load))
    solved = solve(place, load, gathered)
    stress = jnp.einsum("kcu,kus->cs", solved[1], stress_kernel, preferred_element_type=F32)
    arrived = round_y(solved)
    arrived[1], stress = lax.optimization_barrier((arrived[1], stress))
    pieces = []
    for piece in arrived:
        pieces += [piece, swap_cores(piece)]
    parts, solved = lax.optimization_barrier((parts, solved))
    parts = join(parts, outer_round(parts, "zx", 0))
    got = outer_round(parts, "zx", 1)
    factor_slots = [parts[0], got[0], parts[1], got[1]]

    result = outer_product(place, state, pieces, factor_slots)
    return result.reshape(right_side.shape), stress


def solution(mesh):
    in_specs = (P(None, "row", None, "col"), P(None, "row", None, "col", None, None), P(), P(), P())
    out_specs = (P(None, "row", None, "col"), P(("col", "row"), None))
    return jax.shard_map(shards, mesh=mesh, in_specs=in_specs, out_specs=out_specs, check_vma=False)
```

```python
import jax
import jax.numpy as jnp
from jax import lax
from jax.experimental import pallas as pl
from jax.experimental.pallas import tpu as pltpu
from jax.sharding import PartitionSpec as P

STEPS = 8
HALF = STEPS // 2
CHIPS_Y = 4
CORES = 2
BF16 = jnp.bfloat16
F32 = jnp.float32


def dot_nn(a, b):
    return lax.dot_general(a, b, (((1,), (0,)), ((), ())), preferred_element_type=F32)


def dot_nt(a, b):
    return lax.dot_general(a, b, (((1,), (1,)), ((), ())), preferred_element_type=F32)


def upper_chunks():
    chunks = []
    for p in range(STEPS - 1, -1, -1):
        cuts = [p, STEPS] if p >= HALF else [p, HALF, STEPS]
        if p == 0:
            cuts.insert(1, 1)
        chunks += [(p, low, high) for low, high in reversed(list(zip(cuts, cuts[1:])))]
    return chunks


def solve_kernel(place_ref, load_ref, factor_ref, solved_ref, *scratch):
    lower, upper, sems = scratch[: STEPS - 1], scratch[STEPS - 1 : -1], scratch[-1]
    chunks = upper_chunks()
    first = place_ref[0]
    lower_copies = [None]
    for p in range(1, STEPS):
        source = factor_ref.at[lax.rem(first + p, STEPS), :, 0:p]
        lower_copies.append(pltpu.make_async_copy(source, lower[p - 1], sems.at[p - 1]))
        lower_copies[p].start()
    upper_copies = []
    for i, (p, low, high) in enumerate(chunks):
        source = factor_ref.at[lax.rem(first + p, STEPS), :, low:high]
        upper_copies.append(pltpu.make_async_copy(source, upper[i], sems.at[STEPS - 1 + i]))
        upper_copies[i].start()

    def block(ref, k):
        value = ref[:, k]
        return value.reshape(value.shape[0] * value.shape[1], value.shape[2])

    forward = []
    for p in range(STEPS):
        rows = load_ref[lax.rem(first + p, STEPS)]
        if p:
            lower_copies[p].wait()
        for k in range(p):
            rows = rows - dot_nn(forward[k], block(lower[p - 1], k))
        forward.append(rows.astype(BF16))
        solved_ref[0, p] = forward[p]
    back = [None] * STEPS
    rows = None
    for i, (p, low, high) in enumerate(chunks):
        if high == STEPS:
            rows = forward[p].astype(F32)
        upper_copies[i].wait()
        for k in range(high - 1, max(low, p + 1) - 1, -1):
            rows = rows - dot_nn(back[k], block(upper[i], k - low))
        if low == p:
            back[p] = dot_nn(rows.astype(BF16), block(upper[i], 0)).astype(BF16)
            solved_ref[1, p] = back[p]


def solve(place, load, factor):
    _, cases, width = load.shape
    _, slices, _, slice_rows, _ = factor.shape
    blocks_n = STEPS * STEPS
    whole = pl.BlockSpec(memory_space=pltpu.VMEM)
    return pl.pallas_call(
        solve_kernel,
        out_shape=jax.ShapeDtypeStruct((2, STEPS, cases, width), BF16),
        in_specs=[pl.BlockSpec(memory_space=pltpu.SMEM), whole, pl.BlockSpec(memory_space=pl.ANY)],
        out_specs=whole,
        scratch_shapes=[pltpu.VMEM((slices, p, slice_rows, width), BF16) for p in range(1, STEPS)]
        + [pltpu.VMEM((slices, high - low, slice_rows, width), BF16) for _, low, high in upper_chunks()]
        + [pltpu.SemaphoreType.DMA((STEPS - 1 + len(upper_chunks()),))],
        compiler_params=pltpu.CompilerParams(vmem_limit_bytes=40 * 2**20),
        cost_estimate=pl.CostEstimate(
            flops=2 * blocks_n * width * width * cases,
            bytes_accessed=2 * blocks_n * width * width,
            transcendentals=0,
        ),
        name="solve",
    )(place, load, factor)


def origin_xor(bits, core):
    mask = 0
    if bits & 1:
        mask = jnp.where(core == 0, 1, 3)
    if bits & 2:
        mask = mask ^ jnp.where(core == 0, 3, 1)
    return mask


def outer_kernel(place_ref, state_ref, *refs):
    pieces = [refs[2 * chip : 2 * chip + 2] for chip in range(CHIPS_Y)]
    factor_slots = (refs[8:10], refs[10:12])
    out_ref, load, factor, used, solved, load_sem, factor_sem, used_sem, solved_sem = refs[12:]
    first, y, core, z, x = (place_ref[i] for i in range(5))
    row = CORES * y + core
    rank = lax.rem(row - first + STEPS, STEPS)
    inside = lax.div(first + rank, STEPS)
    upper = (row < first).astype(jnp.int32)

    def begin(source, target, sem):
        copy = pltpu.make_async_copy(source, target, sem)
        copy.start()
        return copy

    solved_copies, used_copies, factor_copies = [], [], ([], [])
    for shift in range(CHIPS_Y):
        chip = lax.rem(y - shift + CHIPS_Y, CHIPS_Y)
        for side in range(CORES):
            place = chip * CORES + (core ^ side)
            piece = pieces[shift][side]
            solved_copies.append(begin(piece.at[1, rank], solved.at[place], solved_sem.at[shift, side]))
            used_copies.append(begin(piece.at[upper], used.at[place], used_sem.at[shift, side]))
    used_copies.append(begin(state_ref.at[1 - inside], load, load_sem.at[0]))
    for half in range(2):
        for bits in range(4):
            far = origin_xor(bits, core)
            source = factor_slots[half][bits >> 1].at[pl.ds((bits & 1) * 4, 4)]
            target = factor.at[half, z ^ far] if half == 0 else factor.at[half, :, x ^ far]
            factor_copies[half].append(begin(source, target, factor_sem.at[half, bits]))
    for copy in solved_copies:
        copy.wait()
    panel = solved[...]
    out_ref[inside] = jnp.transpose(panel.reshape(-1, panel.shape[-1]).astype(F32))
    for copy in used_copies:
        copy.wait()
    total = load[...]
    for half in range(2):
        for copy in factor_copies[half]:
            copy.wait()
        for k in range(HALF):
            left = factor[half, :, :, k]
            right = used[:, half * HALF + k]
            total = total - dot_nt(left.reshape(-1, left.shape[-1]), right.reshape(-1, right.shape[-1]))
    out_ref[1 - inside] = total


def outer_product(place, state, pieces, factor_slots):
    _, _, cases, width = pieces[0].shape
    slice_rows = factor_slots[0].shape[2]
    places = CHIPS_Y * CORES
    whole = pl.BlockSpec(memory_space=pltpu.VMEM)
    remote = pl.BlockSpec(memory_space=pl.ANY)
    return pl.pallas_call(
        outer_kernel,
        out_shape=jax.ShapeDtypeStruct(state.shape, F32),
        in_specs=[pl.BlockSpec(memory_space=pltpu.SMEM)] + [remote] * (1 + 2 * CHIPS_Y + 4),
        out_specs=whole,
        scratch_shapes=[
            pltpu.VMEM(state.shape[1:], F32),
            pltpu.VMEM((2, 4, 4, HALF, slice_rows, width), BF16),
            pltpu.VMEM((places, STEPS, cases, width), BF16),
            pltpu.VMEM((places, cases, width), BF16),
            pltpu.SemaphoreType.DMA((1,)),
            pltpu.SemaphoreType.DMA((2, 4)),
            pltpu.SemaphoreType.DMA((CHIPS_Y, CORES)),
            pltpu.SemaphoreType.DMA((CHIPS_Y, CORES)),
        ],
        compiler_params=pltpu.CompilerParams(vmem_limit_bytes=16 * 2**20),
        cost_estimate=pl.CostEstimate(
            flops=2 * STEPS * width * width * places * cases,
            bytes_accessed=2 * STEPS * width * (width + places * cases),
            transcendentals=0,
        ),
        name="outer_product",
    )(place, state, *pieces, *factor_slots)


def pick_kernel(start_ref, owner_ref, parts_ref, out_ref, sems):
    copies = []
    for k in range(STEPS):
        owner = owner_ref[lax.rem(start_ref[0] + k, parts_ref.shape[0])]
        copies.append(pltpu.make_async_copy(parts_ref.at[owner], out_ref.at[k], sems.at[k]))
        copies[k].start()
    for copy in copies:
        copy.wait()


def pick_columns(window_start, col_owner, parts):
    scalars = pl.BlockSpec(memory_space=pltpu.SMEM)
    return pl.pallas_call(
        pick_kernel,
        out_shape=jax.ShapeDtypeStruct((STEPS,) + parts.shape[1:], parts.dtype),
        in_specs=[scalars, scalars, pl.BlockSpec(memory_space=pl.ANY)],
        out_specs=pl.BlockSpec(memory_space=pltpu.VMEM),
        scratch_shapes=[pltpu.SemaphoreType.DMA((STEPS,))],
        cost_estimate=pl.CostEstimate(flops=0, bytes_accessed=64 * parts.size, transcendentals=0),
        name="pick_columns",
    )(window_start, col_owner, parts)


def device_pairs(move):
    pairs = []
    for y in range(4):
        for core in range(2):
            for z in range(4):
                for x in range(4):
                    to_y, to_core, to_z, to_x = move(y, core, z, x)
                    pairs.append(((y * 2 + core) * 16 + z * 4 + x, (to_y * 2 + to_core) * 16 + to_z * 4 + to_x))
    return pairs


def double(value, axis, step):
    masks = (1, 3) if step == 0 else (3, 1)

    def move(y, core, z, x):
        if axis == "x":
            return y, core, z, x ^ masks[core]
        return y, core, z ^ masks[core], x

    return lax.ppermute(value, ("row", "col"), device_pairs(move))


def swap_cores(value):
    return lax.ppermute(value, "row", [(r, r ^ 1) for r in range(CHIPS_Y * CORES)])


def round_y(value):
    rows = [(y, core) for y in range(CHIPS_Y) for core in range(CORES)]
    pieces = [value]
    for shift in range(1, CHIPS_Y):
        pairs = [(y * CORES + core, (y + shift) % CHIPS_Y * CORES + core) for y, core in rows]
        pieces.append(lax.ppermute(value, "row", pairs))
    return pieces


def in_order(part, here, core):
    slots = []
    for coordinate in range(4):
        apart = coordinate ^ here
        slot = apart ^ (apart >> 1)
        slot = jnp.where(core == 0, slot, (slot & 1) * 2 + (slot >> 1))
        slots.append(lax.dynamic_index_in_dim(part, slot, 0, keepdims=False))
    return jnp.stack(slots)


def outer_round(parts, axes, step):
    return [double(part, axis, step) for part, axis in zip(parts, axes)]


def join(parts, got):
    return [jnp.concatenate([part, new]) for part, new in zip(parts, got)]


def shards(right_side, factor_store, col_owner, window_start, stress_kernel):
    rows_n = lax.axis_size("row")
    cols_n = lax.axis_size("col")
    row_id = lax.axis_index("row")
    col_id = lax.axis_index("col")
    core = row_id % CORES
    first = window_start[0]
    panels_dev, _, width, cases = right_side.shape
    own_cases = cases // rows_n
    slice_rows = width // cols_n
    rank = (row_id - first) % rows_n
    inside = (first + rank) // rows_n
    state = right_side.reshape(panels_dev, width, cases)
    factor = factor_store.reshape(panels_dev, width, width)

    def spread(panel):
        parts = lax.all_to_all(panel.reshape(cols_n, slice_rows, width), "col", 0, 0)
        return pick_columns(window_start, col_owner, parts)

    window_factor = jnp.where(inside == 0, factor[0], factor[1])
    outer_factor = jnp.where(inside == 0, factor[1], factor[0])
    window_slices = spread(window_factor.T)
    gathered = lax.all_gather(window_slices, ("row", "col"))
    gathered = gathered.reshape(rows_n, cols_n, STEPS, slice_rows, width)

    outer_factor, state, window_slices = lax.optimization_barrier((outer_factor, state, window_slices))
    window_load = lax.dynamic_index_in_dim(state, inside, 0, keepdims=False)
    load = window_load.T.reshape(rows_n, own_cases, width)
    load = lax.all_to_all(load, "row", 0, 0)
    outer_factor, load = lax.optimization_barrier((outer_factor, load))
    place = jnp.stack([first, row_id // CORES, core, col_id // 4, col_id % 4]).astype(jnp.int32)
    slices = spread(outer_factor)
    parts = [slices[None, :HALF], slices[None, HALF:]]
    parts = join(parts, outer_round(parts, "xz", 0))
    parts = join(parts, outer_round(parts, "xz", 1))
    parts = [in_order(part, here, core) for part, here in zip(parts, (col_id % 4, col_id // 4))]
    parts, gathered, load = lax.optimization_barrier((parts, gathered, load))
    solved = solve(place, load, gathered)
    stress = jnp.einsum("kcu,kus->cs", solved[1], stress_kernel, preferred_element_type=F32)
    arrived = round_y(solved)
    arrived[1], stress = lax.optimization_barrier((arrived[1], stress))
    pieces = []
    for piece in arrived:
        pieces += [piece, swap_cores(piece)]
    parts, solved = lax.optimization_barrier((parts, solved))
    parts = join(parts, outer_round(parts, "zx", 0))
    got = outer_round(parts, "zx", 1)
    factor_slots = [parts[0], got[0], parts[1], got[1]]

    result = outer_product(place, state, pieces, factor_slots)
    return result.reshape(right_side.shape), stress


def solution(mesh):
    in_specs = (P(None, "row", None, "col"), P(None, "row", None, "col", None, None), P(), P(), P())
    out_specs = (P(None, "row", None, "col"), P(("col", "row"), None))
    return jax.shard_map(shards, mesh=mesh, in_specs=in_specs, out_specs=out_specs, check_vma=False)
```
